256 devices in a mesh: gx: 64 (over y, z, x_hi), gy: 4 (over x_lo, core).
Axes of the slice: x: 4 (x_hi: 2, x_lo: 2; x = x_hi * 2 + x_lo), y: 4, z: 8, core: 2. Of those that a mesh axis runs over, the one named last changes fastest.
Arguments:
- layer_input: bfloat16 [128, 128, 32, 512], P('gx', 'gy'), may hold values from -6 to 6
- cotangent: bfloat16 [128, 128, 32, 512], P('gx', 'gy'), may hold values from -6 to 6
- spectral_weight: bfloat16 [32, 64, 32, 1024], P('gy', 'gx'), may hold values from -12 to 12
- bypass_weight: bfloat16 [32, 32], replicated, may hold values from -1 to 1
- channel_bias: float32 [32], replicated, may hold values from -4 to 4
- hash_key: int32 [2], replicated, may hold values from 0 to 1073741823
Outputs:
- grad_input: bfloat16 [128, 128, 32, 512], P('gx', 'gy')
- grad_spectral: float32 [32, 64, 32, 1024], P('gy', 'gx')
- grad_bypass: float32 [32, 32], replicated
- grad_bias: float32 [32], replicated
The draws below stay inside these ranges and needn't reach their ends.
All inputs are finite; a program needn't handle non-finite values.
Results may differ from the reference program's by a relative error of at most 0.011.
Values sent between devices are 32-bit elements; how exact they have to be, the bound alone decides.
No kernel may reach another device: no remote copies, remote signals or barrier semaphores. Data moves between devices by JAX's collectives and lax.ppermute only.
A program may use at most 64 MiB of HBM per device.

```python
import math
import jax
import jax.numpy as jnp
from jax import lax

LX = 128
LY = 128
LZ = 64
LT = 8
C = 32
KX = 32
KY = 32
KZ = 16
KT = 4
LZT = 512
KZT = 64
CC = 1024


def level_of(rng, extent, cuts, smallest, high):
    loudness = 1.0
    for axis_at, shards_of in cuts:
        draws = jax.random.uniform(jax.random.fold_in(jax.random.fold_in(rng, 6), axis_at), (shards_of,), jnp.float32, smallest / len(cuts), high / len(cuts))
        loudness = loudness * jnp.repeat(jnp.exp(draws), extent[axis_at] // shards_of).reshape((-1,) + (1,) * (len(extent) - 1 - axis_at))
    return loudness


def gaussian(stream_key, shape, width, bound, pieces=(), held_as=jnp.bfloat16):
    level = level_of(stream_key, shape, pieces, -0.22, 0.18) if pieces else 1.0
    values = jax.random.normal(stream_key, shape, jnp.float32) * width * level
    return jnp.minimum(jnp.maximum(values, -bound), bound).astype(held_as)


def setup_inputs(seed: int = 0) -> dict:
    seeds = jax.random.split(jax.random.key(seed), 7)
    return {
        "layer_input": gaussian(seeds[0], (LX, LY, C, LZT), 1.0, 6.0, ((0, 64), (1, 4))),
        "cotangent": gaussian(seeds[1], (LX, LY, C, LZT), 1.0, 6.0, ((0, 64), (1, 4))),
        "spectral_weight": gaussian(seeds[2], (KY, KZT, KX, CC), 2.0, 12.0, ((0, 4), (1, 64))),
        "bypass_weight": gaussian(seeds[3], (C, C), C ** -0.5, 1.0),
        "channel_bias": gaussian(seeds[4], (C,), 1.0, 4.0, (), jnp.float32),
        "hash_key": jax.random.randint(seeds[5], (2,), 0, 1073741824).astype(jnp.int32),
    }


keep_level = 6554
keep_scale = 1.0 / 0.9
gelu_cubic = 0.044715
mixer_one = -1640531535
mixer_two = -2048144789
mixer_three = -1028477387

def hartley_table(kept, length):
    wanted = jnp.arange(kept, dtype=jnp.int32)
    frequency = jnp.where(wanted < kept // 2, wanted, wanted + (length - kept))
    positions = jnp.arange(length, dtype=jnp.int32)
    residue = frequency[:, None] * positions[None, :] % length
    radians = residue.astype(jnp.float32) * (2.0 * math.pi / length)
    return (jnp.cos(radians) + jnp.sin(radians)) / math.sqrt(length)

def depth_table():
    depth_part = hartley_table(KZ, LZ)
    time_part = hartley_table(KT, LT)
    joined = depth_part[:, None, :, None] * time_part[None, :, None, :]
    return joined.reshape(KZ * KT, LZ * LT)

def scramble(hashed):
    hashed = jnp.bitwise_xor(hashed, lax.shift_right_logical(hashed, jnp.int32(16)))
    hashed = hashed * jnp.int32(mixer_two)
    hashed = jnp.bitwise_xor(hashed, lax.shift_right_logical(hashed, jnp.int32(13)))
    hashed = hashed * jnp.int32(mixer_three)
    return jnp.bitwise_xor(hashed, lax.shift_right_logical(hashed, jnp.int32(16)))

def dropout_keep(cell_index, hash_key):
    hashed = cell_index * jnp.int32(mixer_one) + hash_key[0]
    hashed = scramble(hashed)
    hashed = scramble(jnp.bitwise_xor(hashed, hash_key[1]))
    return jnp.bitwise_and(hashed, jnp.int32(65535)) >= keep_level

def gelu_slope(preact):
    factor = math.sqrt(2.0 / math.pi)
    tanh_value = jnp.tanh(factor * (preact + gelu_cubic * preact * preact * preact))
    return 0.5 * (1.0 + tanh_value) + 0.5 * preact * (1.0 - tanh_value * tanh_value) * factor * (1.0 + 3.0 * gelu_cubic * preact * preact)

def reference(layer_input, cotangent, spectral_weight, bypass_weight, channel_bias, hash_key):
    highest = lax.Precision.HIGHEST
    across_table = hartley_table(KX, LX)
    down_table = hartley_table(KY, LY)
    depth_full = depth_table()
    depth_low = depth_full.T.astype(jnp.bfloat16)
    weight_modes = spectral_weight.astype(jnp.float32).reshape(KY, KZT, KX, C, C)
    bypass_wide = bypass_weight.astype(jnp.float32)

    def forward_modes(source):

        def one_plane(plane):
            depth_part = jnp.dot(plane.reshape(LY * C, LZT), depth_low, preferred_element_type=jnp.float32)
            return jnp.einsum('ky,ycm->kcm', down_table, depth_part.reshape(LY, C, KZT), precision=highest)
        planes = lax.map(one_plane, source)
        return jnp.einsum('jx,xkcm->jkcm', across_table, planes, precision=highest)

    def plane_cells(plane_modes):
        column_modes = jnp.einsum('ky,kcm->ycm', down_table, plane_modes, precision=highest)
        flattened = jnp.dot(column_modes.reshape(LY * C, KZT), depth_full, precision=highest, preferred_element_type=jnp.float32)
        return flattened.reshape(LY, C, LZT)
    column_ids = jnp.arange(LY, dtype=jnp.int32)
    channel_ids = jnp.arange(C, dtype=jnp.int32)
    depth_ids = jnp.arange(LZT, dtype=jnp.int32)
    plane_ids = jnp.arange(LX, dtype=jnp.int32)
    input_modes = forward_modes(layer_input)
    mixed_modes = jnp.einsum('jkcm,kmjcd->jkdm', input_modes, weight_modes, precision=highest)
    spread = jnp.einsum('jx,jkcm->xkcm', across_table, mixed_modes, precision=highest)

    def first_pass(plane_items):
        plane_modes, plane, cot_plane, plane_row = plane_items
        spectral = plane_cells(plane_modes)
        bypass = jnp.einsum('yct,cd->ydt', plane.astype(jnp.float32), bypass_wide, precision=highest)
        preact = spectral + bypass + channel_bias[None, :, None]
        cell_index = ((plane_row * LY + column_ids[:, None, None]) * C + channel_ids[None, :, None]) * LZT + depth_ids[None, None, :]
        keep_mask = dropout_keep(cell_index, hash_key)
        dpre = jnp.where(keep_mask, cot_plane.astype(jnp.float32) * gelu_slope(preact) * keep_scale, 0.0).astype(jnp.bfloat16)
        wide_dpre = dpre.astype(jnp.float32)
        weight_part = jnp.einsum('yct,ydt->cd', plane.astype(jnp.float32), wide_dpre, precision=highest)
        bias_part = lax.optimization_barrier(jnp.sum(wide_dpre, axis=(0, 2)))
        return (dpre, weight_part, bias_part)
    dpre, weight_parts, bias_parts = lax.map(first_pass, (spread, layer_input, cotangent, plane_ids))
    norm_scale = 1.0 / math.sqrt(LX * LY * LZT)
    grad_bypass = lax.optimization_barrier(jnp.sum(weight_parts, axis=0)) * norm_scale
    grad_bias = lax.optimization_barrier(jnp.sum(bias_parts, axis=0)) * norm_scale
    dpre_modes = forward_modes(dpre)
    grad_spectral = jnp.einsum('jkcm,jkdm->kmjcd', input_modes, dpre_modes, precision=highest).reshape(KY, KZT, KX, C * C)
    backward_modes = jnp.einsum('jkdm,kmjcd->jkcm', dpre_modes, weight_modes, precision=highest)
    spread_back = jnp.einsum('jx,jkcm->xkcm', across_table, backward_modes, precision=highest)

    def second_pass(plane_items):
        plane_modes, dpre_plane = plane_items
        local_part = jnp.einsum('ydt,cd->yct', dpre_plane.astype(jnp.float32), bypass_wide, precision=highest)
        return (plane_cells(plane_modes) + local_part).astype(jnp.bfloat16)
    grad_input = lax.map(second_pass, (spread_back, dpre))
    return (grad_input, grad_spectral, grad_bypass, grad_bias)
```

```python
import functools
import math

import jax
import jax.numpy as jnp
import numpy as np
from jax import lax
from jax.experimental import pallas as pl
from jax.experimental.pallas import tpu as pltpu
from jax.sharding import PartitionSpec as P

LX = 128
LY = 128
LZ = 64
LT = 8
KX = 32
KY = 32
KZ = 16
KT = 4
C = 32
LZT = 512
KZT = 64
GX = 64
GY = 4
ROWS = 256
F32 = jnp.float32
BF16 = jnp.bfloat16
HIGHEST = lax.Precision.HIGHEST

keep_level = 6554
keep_scale = 1.0 / 0.9
gelu_cubic = 0.044715
mixer_one = -1640531535
mixer_two = -2048144789
mixer_three = -1028477387
norm_scale = 1.0 / math.sqrt(LX * LY * LZT)


def hartley_table(kept, length):
    wanted = np.arange(kept)
    frequency = np.where(wanted < kept // 2, wanted, wanted + (length - kept))
    residue = frequency[:, None] * np.arange(length)[None, :] % length
    radians = residue * (2.0 * math.pi / length)
    return ((np.cos(radians) + np.sin(radians)) / math.sqrt(length)).astype(np.float32)


def depth_table():
    joined = hartley_table(KZ, LZ)[:, None, :, None] * hartley_table(KT, LT)[None, :, None, :]
    return joined.reshape(KZT, LZT)


def split_table(table):
    high = table.astype(jnp.bfloat16)
    return high, (table - high.astype(np.float32)).astype(jnp.bfloat16)


def down_by_device():
    down = hartley_table(KY, LY)
    picked = []
    for q in range(GY):
        order = [
            ((side * 2 + (q % 2 + swap) % 2) * 8 + k)
            for swap in range(2)
            for side in range(2)
            for k in range(8)
        ]
        picked.append(down[order][:, q * 32 : (q + 1) * 32])
    return np.stack(picked)


def tables():
    down = down_by_device()
    spread = lambda t: np.repeat(t, C, axis=2)
    depth = depth_table()
    depth_high, depth_rest = split_table(depth)
    across = hartley_table(KX, LX)
    gather = np.concatenate([np.repeat(across[:, x::2], 2, axis=1) for x in range(2)], axis=1)
    scatter = np.concatenate([across[:, x::2].T for x in range(2)], axis=0)
    eye = np.eye(C, dtype=np.float32)
    return dict(
        down_cells=spread(down.transpose(0, 2, 1)),
        down_modes=spread(down),
        depth_low=depth_high,
        depth_stack=np.concatenate([depth_high, depth_high, depth_rest], axis=0),
        gather=gather,
        scatter=scatter,
        expand=np.concatenate([np.repeat(eye, C, axis=1)] * 2, axis=0).astype(jnp.bfloat16),
        tile4=np.concatenate([np.tile(eye, (1, 4))] * 2, axis=0).astype(jnp.bfloat16),
        fold4=np.concatenate([np.tile(eye, (4, 8))] * 2, axis=0).astype(jnp.bfloat16),
        fold32=np.tile(np.repeat(eye, C, axis=0), (1, 8)).astype(jnp.bfloat16),
        fold8=np.concatenate([np.tile(eye, (8, 1)), np.zeros((256, 96), np.float32)], axis=1),
    )


def halves(value):
    high = value.astype(BF16)
    return high, (value - high.astype(F32)).astype(BF16)


def mm(a, b):
    return jnp.dot(a, b, preferred_element_type=F32)


def mm_nt(a, b):
    return lax.dot_general(a, b, (((1,), (1,)), ((), ())), preferred_element_type=F32)


def mm_tn(a, b):
    return lax.dot_general(a, b, (((0,), (0,)), ((), ())), preferred_element_type=F32)


def build_spread(table_ref, high_ref, rest_ref):
    q = lax.axis_index("gy")
    shape = (C, 32 * C)
    mask = lax.broadcasted_iota(jnp.int32, shape, 0) == (
        lax.broadcasted_iota(jnp.int32, shape, 1) & (C - 1)
    )
    for row in range(32):
        line = table_ref[q, pl.ds(row, 1), :]
        value = jnp.where(mask, line, 0.0)
        high, rest = halves(value)
        high_ref[pl.ds(row * C, C), :] = high
        rest_ref[pl.ds(row * C, C), :] = rest


def times_spread(value, high_ref, rest_ref):
    high, rest = halves(value)
    return mm(high, high_ref[...]) + mm(rest, high_ref[...]) + mm(high, rest_ref[...])


def send_modes(modes, own_ref, other_ref, lines):
    for swap, ref in enumerate((own_ref, other_ref)):
        for side in range(2):
            for x in range(2):
                for half in range(2):
                    at = ((swap * 2 + side) * 2 + half) * 128
                    ref[pl.ds(side * lines + x * 2 + half, KZT, stride=2 * lines), :] = modes[
                        x * KZT : (x + 1) * KZT, at : at + 128
                    ]


def received_modes(own_ref, other_ref, lines):
    rows = []
    for x in range(2):
        parts = []
        for ref in (own_ref, other_ref):
            for side in range(2):
                for half in range(2):
                    parts.append(ref[pl.ds(side * lines + x * 2 + half, KZT, stride=2 * lines), :])
        rows.append(jnp.concatenate(parts, axis=1))
    return jnp.concatenate(rows, axis=0)


def block_mixing(weight_ref):
    weight = weight_ref[...].astype(F32)
    wide = jnp.concatenate([weight] * 8, axis=1)
    full = jnp.concatenate([wide] * 8, axis=0)
    shape = (ROWS, ROWS)
    same = (lax.broadcasted_iota(jnp.int32, shape, 0) >> 5) == (
        lax.broadcasted_iota(jnp.int32, shape, 1) >> 5
    )
    return jnp.where(same, full, 0.0)


def fill_inverse(own_ref, other_ref, lines, down_ref, high_ref, rest_ref, stack_ref):
    build_spread(down_ref, high_ref, rest_ref)
    cells = times_spread(received_modes(own_ref, other_ref, lines), high_ref, rest_ref)
    high, rest = halves(cells)
    for x in range(2):
        part = slice(x * KZT, (x + 1) * KZT)
        stack_ref[x, 0:KZT, :] = high[part]
        stack_ref[x, KZT : 2 * KZT, :] = rest[part]
        stack_ref[x, 2 * KZT : 3 * KZT, :] = high[part]


def forward_kernel(field, depth_low, down, own, other, flat, high, rest):
    step = pl.program_id(0)

    @pl.when(step == 0)
    def _():
        build_spread(down, high, rest)

    x, block = step // 4, step % 4
    flat[x, block] = mm_nt(depth_low[...], field[...])

    @pl.when(step == 7)
    def _():
        send_modes(times_spread(joined(flat), high, rest), own, other, 4)


def joined(flat):
    return jnp.concatenate(
        [jnp.concatenate([flat[x, block] for block in range(4)], axis=1) for x in range(2)], axis=0
    )


def scramble(hashed):
    hashed = jnp.bitwise_xor(hashed, lax.shift_right_logical(hashed, jnp.int32(16)))
    hashed = hashed * jnp.int32(mixer_two)
    hashed = jnp.bitwise_xor(hashed, lax.shift_right_logical(hashed, jnp.int32(13)))
    hashed = hashed * jnp.int32(mixer_three)
    return jnp.bitwise_xor(hashed, lax.shift_right_logical(hashed, jnp.int32(16)))


def dropout_kernel(key, cotangent, kept):
    step = pl.program_id(0)
    x, block = step // 4, step % 4
    plane = lax.axis_index("gx") * 2 + x
    column = lax.axis_index("gy") * 32 + block * 8
    first = (plane * LY + column) * (C * LZT)
    shape = (16, LZT)
    inside = (
        lax.broadcasted_iota(jnp.int32, shape, 0) * LZT + lax.broadcasted_iota(jnp.int32, shape, 1)
    ) * jnp.int32(mixer_one)

    def body(chunk, carry):
        start = (first + chunk * (16 * LZT)) * jnp.int32(mixer_one) + key[0]
        hashed = scramble(inside + start)
        hashed = scramble(jnp.bitwise_xor(hashed, key[1]))
        keep = jnp.bitwise_and(hashed, jnp.int32(65535)) >= keep_level
        rows = pl.ds(pl.multiple_of(chunk * 16, 16), 16)
        kept[rows, :] = jnp.where(keep, cotangent[rows, :].astype(F32), 0.0).astype(BF16)
        return carry

    lax.fori_loop(0, ROWS // 16, body, 0)


def gathered_modes(messages, gather, lines):
    slabs = [
        jnp.concatenate([messages[pl.ds(x * 2 + half, 128, stride=lines), :] for half in range(2)], axis=1)
        for x in range(2)
    ]
    return jnp.dot(gather[...], jnp.concatenate(slabs, axis=0), precision=HIGHEST, preferred_element_type=F32)


def by_mode(modes):
    return jnp.concatenate([modes[:, k * C : (k + 1) * C] for k in range(8)], axis=0)


def wide_halves(value):
    return jnp.concatenate(halves(value), axis=1)


def scatter_planes(repeated, scatter, out, lines):
    lane = lax.broadcasted_iota(jnp.int32, (KX, ROWS), 1) >> 5
    modes = jnp.zeros((KX, ROWS), F32)
    for k in range(8):
        modes = jnp.where(lane == k, repeated[k * KX : (k + 1) * KX, :], modes)
    planes = jnp.dot(scatter[...], modes, precision=HIGHEST, preferred_element_type=F32)
    for x in range(2):
        for half in range(2):
            piece = planes[x * GX : (x + 1) * GX, half * 128 : (half + 1) * 128]
            for side in range(2):
                out[pl.ds(side * lines + x * 2 + half, GX, stride=2 * lines), :] = piece


def mix_kernel(messages, weight, gather, scatter, expand, fold4, out, modes_out):
    modes = gathered_modes(messages, gather, 4)
    modes_out[...] = modes
    spread = mm(wide_halves(by_mode(modes)), expand[...])
    total = jnp.zeros((ROWS, 128), F32)
    for j in range(8):
        part = slice(j * 128, (j + 1) * 128)
        total = total + spread[:, part] * weight[:, part].astype(F32)
    repeated = mm(wide_halves(total), fold4[...])
    scatter_planes(repeated, scatter, out, 4)


def back_kernel(messages, modes, weight, gather, scatter, expand, tile4, fold32, out, grad):
    dmodes = wide_halves(by_mode(gathered_modes(messages, gather, 5)))
    tiled = mm(dmodes, tile4[...])
    spread = mm(wide_halves(by_mode(modes[...])), expand[...])
    repeated = jnp.zeros((ROWS, ROWS), F32)
    for j in range(8):
        part = slice(j * 128, (j + 1) * 128)
        grad[:, part] = spread[:, part] * tiled
        high, rest = halves(weight[:, part].astype(F32) * tiled)
        repeated = repeated + mm(high, fold32[part, :]) + mm(rest, fold32[part, :])
    scatter_planes(repeated, scatter, out, 5)
    total = jnp.sum(messages[pl.ds(4, 128, stride=5), :], axis=0, keepdims=True)
    out[pl.ds(4, 128, stride=5), :] = jnp.broadcast_to(total, (128, 128))


def gelu_slope(preact):
    factor = math.sqrt(2.0 / math.pi)
    square = preact * preact
    tanh_value = jnp.tanh(preact * (factor + (factor * gelu_cubic) * square))
    rest = preact * (0.5 * factor + (1.5 * factor * gelu_cubic) * square)
    return 0.5 + 0.5 * tanh_value + rest * (1.0 - tanh_value * tanh_value)


def middle_kernel(
    own_in, other_in, field, kept, bias, bypass, depth_stack, depth_low, down_modes, down_cells, fold8,
    dpre, own, other,
    high_in, rest_in, high, rest, stack, mixing, preact, flat, sums, bias_sums,
):
    step = pl.program_id(0)
    x, block = step // 4, step % 4

    @pl.when(step == 0)
    def _():
        fill_inverse(own_in, other_in, 4, down_modes, high_in, rest_in, stack)
        build_spread(down_cells, high, rest)
        mixing[...] = jnp.transpose(block_mixing(bypass)).astype(BF16)
        sums[...] = jnp.zeros_like(sums)
        bias_sums[...] = jnp.zeros_like(bias_sums)

    columns = pl.ds(pl.multiple_of(block * ROWS, ROWS), ROWS)
    preact[...] = mm_tn(stack[x, :, columns], depth_stack[...]) + mm(mixing[...], field[...])

    def body(chunk, carry):
        rows = pl.ds(pl.multiple_of(chunk * 16, 16), 16)
        shift = bias[pl.ds(pl.multiple_of((chunk % 2) * 16, 16), 16), :]
        slope = gelu_slope(preact[rows, :] + shift)
        dpre[rows, :] = (kept[rows, :].astype(F32) * slope * keep_scale).astype(BF16)
        return carry

    lax.fori_loop(0, ROWS // 16, body, 0)
    flat[x, block] = mm_nt(depth_low[...], dpre[...])
    sums[...] += mm_nt(field[...], dpre[...])
    bias_sums[...] += mm_nt(jnp.ones((16, LZT), BF16), dpre[...])

    @pl.when(step == 7)
    def _():
        send_modes(times_spread(joined(flat), high, rest), own, other, 5)
        lane = lax.broadcasted_iota(jnp.int32, (C, ROWS), 1) >> 5
        picked = jnp.zeros((C, ROWS), F32)
        for k in range(8):
            picked = jnp.where(lane == k, sums[k * C : (k + 1) * C, :], picked)
        both = jnp.concatenate([picked, bias_sums[...], jnp.zeros((16, ROWS), F32)], axis=0)
        folded = jnp.dot(both, fold8[...], precision=HIGHEST, preferred_element_type=F32)
        for side in range(2):
            own[pl.ds(side * 5 + 4, KZT, stride=10), :] = folded
            other[pl.ds(side * 5 + 4, KZT, stride=10), :] = jnp.zeros((KZT, 128), F32)


def last_kernel(
    own_in, other_in, dpre, bypass, depth_stack, down_modes,
    grad, grad_weight, grad_bias,
    high_in, rest_in, stack, mixing,
):
    step = pl.program_id(0)
    x, block = step // 4, step % 4

    @pl.when(step == 0)
    def _():
        fill_inverse(own_in, other_in, 5, down_modes, high_in, rest_in, stack)
        mixing[...] = block_mixing(bypass).astype(BF16)
        total = own_in[pl.ds(4, KZT, stride=10), :] + other_in[pl.ds(4, KZT, stride=10), :]
        total = total * norm_scale
        grad_weight[...] = total[0:C, 0:C]
        grad_bias[...] = total[C : C + 8, 0:C]

    columns = pl.ds(pl.multiple_of(block * ROWS, ROWS), ROWS)
    grad[...] = (mm_tn(stack[x, :, columns], depth_stack[...]) + mm(mixing[...], dpre[...])).astype(BF16)


def whole(shape):
    return pl.BlockSpec(shape, lambda *_: (0,) * len(shape))


def rows_block():
    return pl.BlockSpec((ROWS, LZT), lambda i: (i, 0))


SMEM = pl.BlockSpec(memory_space=pltpu.SMEM)
PARAMS = pltpu.CompilerParams(vmem_limit_bytes=48 * 1024 * 1024)


def like(*shape, dtype=F32):
    return jax.ShapeDtypeStruct(shape, dtype)


def call(kernel, name, grid, ins, outs, scratch, out_shape):
    return pl.pallas_call(
        kernel,
        name=name,
        grid=grid,
        in_specs=ins,
        out_specs=outs,
        out_shape=out_shape,
        scratch_shapes=scratch,
        compiler_params=PARAMS,
    )


def swap_cores(value):
    return lax.ppermute(value, "gy", [(i, i ^ 1) for i in range(GY)])


def exchange(messages, lines):
    groups = [[(g * 2 + side) * 2 + core for g in range(GX) for side in range(2)] for core in range(2)]
    shaped = messages.reshape(128, 1, lines * 128)
    moved = lax.all_to_all(
        shaped, ("gx", "gy"), split_axis=0, concat_axis=0, tiled=True, axis_index_groups=groups
    )
    return moved.reshape(128 * lines, 128)


def local(layer_input, cotangent, spectral_weight, bypass_weight, channel_bias, hash_key):
    table = {name: jnp.asarray(value) for name, value in tables().items()}
    field = layer_input.reshape(-1, LZT)
    weight = spectral_weight.reshape(ROWS, C * C)
    square = lambda: pltpu.VMEM((1024, 1024), BF16)
    flat = pltpu.VMEM((2, 4, KZT, ROWS), F32)
    stack = pltpu.VMEM((2, 3 * KZT, 1024), BF16)

    own, other = call(
        forward_kernel,
        "forward",
        (8,),
        [rows_block(), whole((KZT, LZT)), whole((GY, 32, 1024))],
        [whole((512, 128))] * 2,
        [flat, square(), square()],
        [like(512, 128)] * 2,
    )(field, table["depth_low"], table["down_cells"])
    messages = exchange(own + swap_cores(other), 4)

    kept = call(
        dropout_kernel, "dropout", (8,), [SMEM, rows_block()], rows_block(), [], like(2048, LZT, dtype=BF16)
    )(hash_key, cotangent.reshape(-1, LZT))

    planes, modes = call(
        mix_kernel,
        "mix",
        (1,),
        [whole((512, 128)), whole((ROWS, 1024)), whole((32, 256)), whole((128, 32)), whole((64, 1024)), whole((256, 256))],
        [whole((512, 128)), whole((KX, ROWS))],
        [],
        [like(512, 128), like(KX, ROWS)],
    )(messages, weight, table["gather"], table["scatter"], table["expand"], table["fold4"])
    own_cells = exchange(planes, 4)
    other_cells = swap_cores(own_cells)

    wide_bias = jnp.broadcast_to(channel_bias[:, None], (C, LZT))
    dpre, own, other = call(
        middle_kernel,
        "middle",
        (8,),
        [
            whole((512, 128)), whole((512, 128)), rows_block(), rows_block(), whole((C, LZT)), whole((C, C)),
            whole((192, LZT)), whole((KZT, LZT)), whole((GY, 32, 1024)), whole((GY, 32, 1024)), whole((256, 128)),
        ],
        [rows_block(), whole((640, 128)), whole((640, 128))],
        [
            square(), square(), square(), square(), stack,
            pltpu.VMEM((ROWS, ROWS), BF16), pltpu.VMEM((ROWS, LZT), F32), flat,
            pltpu.VMEM((ROWS, ROWS), F32), pltpu.VMEM((16, ROWS), F32),
        ],
        [like(2048, LZT, dtype=BF16), like(640, 128), like(640, 128)],
    )(
        own_cells, other_cells, field, kept, wide_bias, bypass_weight,
        table["depth_stack"], table["depth_low"], table["down_modes"], table["down_cells"], table["fold8"],
    )
    messages = exchange(own + swap_cores(other), 5)

    planes, grad_spectral = call(
        back_kernel,
        "back",
        (1,),
        [
            whole((640, 128)), whole((KX, ROWS)), whole((ROWS, 1024)), whole((32, 256)), whole((128, 32)),
            whole((64, 1024)), whole((64, 128)), whole((1024, 256)),
        ],
        [whole((640, 128)), whole((ROWS, 1024))],
        [],
        [like(640, 128), like(ROWS, 1024)],
    )(
        messages, modes, weight, table["gather"], table["scatter"], table["expand"], table["tile4"], table["fold32"]
    )
    own_cells = exchange(planes, 5)
    other_cells = swap_cores(own_cells)

    grad_input, grad_weight, grad_bias = call(
        last_kernel,
        "last",
        (8,),
        [whole((640, 128)), whole((640, 128)), rows_block(), whole((C, C)), whole((192, LZT)), whole((GY, 32, 1024))],
        [rows_block(), whole((C, C)), whole((8, C))],
        [square(), square(), stack, pltpu.VMEM((ROWS, ROWS), BF16)],
        [like(2048, LZT, dtype=BF16), like(C, C), like(8, C)],
    )(own_cells, other_cells, dpre, bypass_weight, table["depth_stack"], table["down_modes"])
    return (
        grad_input.reshape(layer_input.shape),
        grad_spectral.reshape(spectral_weight.shape),
        grad_weight,
        grad_bias[0],
    )


def solution(mesh):
    return jax.shard_map(
        local,
        mesh=mesh,
        in_specs=(
            P("gx", "gy", None, None),
            P("gx", "gy", None, None),
            P("gy", "gx", None, None),
            P(),
            P(),
            P(),
        ),
        out_specs=(P("gx", "gy", None, None), P("gy", "gx", None, None), P(), P()),
        check_vma=False,
    )
```

```python
import math

import jax
import jax.numpy as jnp
import numpy as np
from jax import lax
from jax.experimental import pallas as pl
from jax.experimental.pallas import tpu as pltpu
from jax.sharding import PartitionSpec as P

LX = 128
LY = 128
LZ = 64
LT = 8
KX = 32
KY = 32
KZ = 16
KT = 4
C = 32
LZT = 512
KZT = 64
GX = 64
GY = 4
ROWS = 256
F32 = jnp.float32
BF16 = jnp.bfloat16
HIGHEST = lax.Precision.HIGHEST

keep_level = 6554
keep_scale = 1.0 / 0.9
gelu_cubic = 0.044715
mixer_one = -1640531535
mixer_two = -2048144789
mixer_three = -1028477387
norm_scale = 1.0 / math.sqrt(LX * LY * LZT)


def hartley_table(kept, length):
    wanted = np.arange(kept)
    frequency = np.where(wanted < kept // 2, wanted, wanted + (length - kept))
    residue = frequency[:, None] * np.arange(length)[None, :] % length
    radians = residue * (2.0 * math.pi / length)
    return ((np.cos(radians) + np.sin(radians)) / math.sqrt(length)).astype(np.float32)


def depth_table():
    joined = hartley_table(KZ, LZ)[:, None, :, None] * hartley_table(KT, LT)[None, :, None, :]
    return joined.reshape(KZT, LZT)


def split_table(table):
    high = table.astype(jnp.bfloat16)
    return high, (table - high.astype(np.float32)).astype(jnp.bfloat16)


def down_by_device():
    down = hartley_table(KY, LY)
    picked = []
    for q in range(GY):
        order = [
            ((side * 2 + (q % 2 + swap) % 2) * 8 + k)
            for swap in range(2)
            for side in range(2)
            for k in range(8)
        ]
        picked.append(down[order][:, q * 32 : (q + 1) * 32])
    return np.stack(picked)


def tables():
    down = down_by_device()
    pair = lambda t: np.concatenate(split_table(t), axis=1)
    depth = depth_table()
    depth_high, depth_rest = split_table(depth)
    across = hartley_table(KX, LX)
    gather = np.concatenate([np.repeat(across[:, x::2], 2, axis=1) for x in range(2)], axis=1)
    scatter = np.concatenate([across[:, x::2] for x in range(2)], axis=1)
    ones = np.concatenate([np.ones((3, LZT)), np.zeros((13, LZT))]).astype(jnp.bfloat16)
    return dict(
        down_cells=pair(down.transpose(0, 2, 1)),
        down_modes=pair(down),
        depth=np.concatenate([depth_high, depth_high, depth_rest, ones], axis=0),
        across=np.concatenate([gather, scatter], axis=1),
    )


def halves(value):
    high = value.astype(BF16)
    return high, (value - high.astype(F32)).astype(BF16)


def mm(a, b):
    return jnp.dot(a, b, preferred_element_type=F32)


def mm_nt(a, b):
    return lax.dot_general(a, b, (((1,), (1,)), ((), ())), preferred_element_type=F32)


def mm_tn(a, b):
    return lax.dot_general(a, b, (((0,), (0,)), ((), ())), preferred_element_type=F32)


def same(shape, rows, columns):
    row_ids = lax.broadcasted_iota(jnp.int32, shape, 0)
    column_ids = lax.broadcasted_iota(jnp.int32, shape, 1)
    return rows(row_ids) == columns(column_ids)


def ones_where(shape, rows, columns, dtype=BF16):
    return jnp.where(same(shape, rows, columns), 1.0, 0.0).astype(dtype)


def channel(index):
    return index & (C - 1)


def group(index):
    return index >> 5


def build_spread(table_ref, wide_ref, high_ref, rest_ref):
    wide_ref[...] = mm(table_ref[lax.axis_index("gy")], ones_where((C, 32 * C), lambda i: i, group))
    mask = same((C, 32 * C), lambda i: i, channel)
    for row in range(32):
        high_ref[row * C : (row + 1) * C, :] = jnp.where(mask, wide_ref[row : row + 1, :], 0.0).astype(BF16)
        rest_ref[row * C : (row + 1) * C, :] = jnp.where(mask, wide_ref[32 + row : 33 + row, :], 0.0).astype(BF16)


def start_copies(pairs, sems):
    copies = [pltpu.make_async_copy(source, target, sems.at[i]) for i, (source, target) in enumerate(pairs)]
    for copy in copies:
        copy.start()
    return copies


def times_spread(value, high_ref, rest_ref):
    high, rest = halves(value)
    return mm(high, high_ref[...]) + mm(rest, high_ref[...]) + mm(high, rest_ref[...])


def send_modes(modes, own_ref, other_ref, lines):
    for swap, ref in enumerate((own_ref, other_ref)):
        for side in range(2):
            for x in range(2):
                for half in range(2):
                    at = ((swap * 2 + side) * 2 + half) * 128
                    ref[pl.ds(side * lines + x * 2 + half, KZT, stride=2 * lines), :] = modes[
                        x * KZT : (x + 1) * KZT, at : at + 128
                    ]


def received_modes(own_ref, other_ref, lines):
    rows = []
    for x in range(2):
        parts = []
        for ref in (own_ref, other_ref):
            for side in range(2):
                for half in range(2):
                    parts.append(ref[pl.ds(side * lines + x * 2 + half, KZT, stride=2 * lines), :])
        rows.append(jnp.concatenate(parts, axis=1))
    return jnp.concatenate(rows, axis=0)


def block_mixing(weight_ref):
    weight = weight_ref[...].astype(F32)
    wide = jnp.concatenate([weight] * 8, axis=1)
    full = jnp.concatenate([wide] * 8, axis=0)
    return jnp.where(same((ROWS, ROWS), group, group), full, 0.0)


def fill_inverse(own_ref, other_ref, lines, high_ref, rest_ref, stack_ref):
    cells = times_spread(received_modes(own_ref, other_ref, lines), high_ref, rest_ref)
    high, rest = halves(cells)
    for x in range(2):
        part = slice(x * KZT, (x + 1) * KZT)
        stack_ref[x, 0:KZT, :] = high[part]
        stack_ref[x, KZT : 2 * KZT, :] = rest[part]
        stack_ref[x, 2 * KZT : 3 * KZT, :] = high[part]


def block_rows(i):
    return slice(i * ROWS, (i + 1) * ROWS)


def block_pairs(source, target):
    return [(source.at[pl.ds(i * ROWS, ROWS)], target.at[pl.ds(i * ROWS, ROWS)]) for i in range(8)]


def forward_kernel(field_in, depth_in, down_in, own, other, field, depth, down, wide, high, rest, flat, sems):
    copies = start_copies(
        [(down_in, down), (depth_in.at[pl.ds(0, KZT)], depth)] + block_pairs(field_in, field), sems
    )
    copies[0].wait()
    build_spread(down, wide, high, rest)
    copies[1].wait()
    for i in range(8):
        copies[2 + i].wait()
        flat[i // 4, i % 4] = mm_nt(depth[...], field[block_rows(i), :])
    send_modes(times_spread(joined(flat), high, rest), own, other, 4)


def joined(flat):
    return jnp.concatenate(
        [jnp.concatenate([flat[x, block] for block in range(4)], axis=1) for x in range(2)], axis=0
    )


def scramble(hashed):
    hashed = jnp.bitwise_xor(hashed, lax.shift_right_logical(hashed, jnp.int32(16)))
    hashed = hashed * jnp.int32(mixer_two)
    hashed = jnp.bitwise_xor(hashed, lax.shift_right_logical(hashed, jnp.int32(13)))
    hashed = hashed * jnp.int32(mixer_three)
    return jnp.bitwise_xor(hashed, lax.shift_right_logical(hashed, jnp.int32(16)))


def prepare_kernel(key, cotangent_in, kept_out, cotangent, kept, in_sems, out_sems):
    arriving = start_copies(block_pairs(cotangent_in, cotangent), in_sems)
    leaving = [pltpu.make_async_copy(source, target, out_sems.at[i]) for i, (source, target) in enumerate(block_pairs(kept, kept_out))]
    origin = (lax.axis_index("gx") * 2 * LY + lax.axis_index("gy") * 32) * (C * LZT)
    shape = (16, LZT)
    inside = (
        lax.broadcasted_iota(jnp.int32, shape, 0) * LZT + lax.broadcasted_iota(jnp.int32, shape, 1)
    ) * jnp.int32(mixer_one)
    for i in range(8):
        first = origin + ((i // 4) * LY + (i % 4) * 8) * (C * LZT)
        arriving[i].wait()

        def body(chunk, carry):
            for part in range(4):
                at = chunk * 64 + part * 16
                start = (first + at * LZT) * jnp.int32(mixer_one) + key[0]
                hashed = scramble(inside + start)
                hashed = scramble(jnp.bitwise_xor(hashed, key[1]))
                keep = jnp.bitwise_and(hashed, jnp.int32(65535)) >= keep_level
                rows = pl.ds(pl.multiple_of(i * ROWS + at, 16), 16)
                kept[rows, :] = jnp.where(keep, cotangent[rows, :].astype(F32), 0.0).astype(BF16)
            return carry

        lax.fori_loop(0, 4, body, 0)
        leaving[i].start()
    for copy in leaving:
        copy.wait()


def gathered_modes(messages, across, lines):
    slabs = [
        jnp.concatenate([messages[pl.ds(x * 2 + half, 128, stride=lines), :] for half in range(2)], axis=1)
        for x in range(2)
    ]
    slabs = jnp.concatenate(slabs, axis=0)
    return jnp.dot(across[:, 0:256], slabs, precision=HIGHEST, preferred_element_type=F32)


def by_mode(modes):
    return jnp.concatenate([modes[:, k * C : (k + 1) * C] for k in range(8)], axis=0)


def wide_halves(value):
    return jnp.concatenate(halves(value), axis=1)


def scatter_planes(repeated, across, out, lines):
    lane = lax.broadcasted_iota(jnp.int32, (KX, ROWS), 1) >> 5
    modes = jnp.zeros((KX, ROWS), F32)
    for k in range(8):
        modes = jnp.where(lane == k, repeated[k * KX : (k + 1) * KX, :], modes)
    planes = lax.dot_general(
        across[:, 256:384], modes, (((0,), (0,)), ((), ())), precision=HIGHEST, preferred_element_type=F32
    )
    for x in range(2):
        for half in range(2):
            piece = planes[x * GX : (x + 1) * GX, half * 128 : (half + 1) * 128]
            for side in range(2):
                out[pl.ds(side * lines + x * 2 + half, GX, stride=2 * lines), :] = piece


def mix_kernel(messages, weight, across, out, modes_out):
    modes = gathered_modes(messages, across, 4)
    modes_out[...] = modes
    spread = mm(wide_halves(by_mode(modes)), ones_where((2 * C, C * C), channel, group))
    total = jnp.zeros((ROWS, 128), F32)
    for j in range(8):
        part = slice(j * 128, (j + 1) * 128)
        total = total + spread[:, part] * weight[:, part].astype(F32)
    repeated = mm(wide_halves(total), ones_where((256, 256), channel, channel))
    scatter_planes(repeated, across, out, 4)


def back_kernel(messages, modes, weight, across, out, grad_out, grad, sems):
    dmodes = wide_halves(by_mode(gathered_modes(messages, across, 5)))
    tiled = mm(dmodes, ones_where((2 * C, 128), channel, channel))
    spread = mm(wide_halves(by_mode(modes[...])), ones_where((2 * C, C * C), channel, group))
    repeated = jnp.zeros((ROWS, ROWS), F32)
    leaving = []
    for j in range(8):
        part = slice(j * 128, (j + 1) * 128)
        grad[:, part] = spread[:, part] * tiled
        copy = pltpu.make_async_copy(
            grad.at[:, pl.ds(j * 128, 128)], grad_out.at[:, pl.ds(j * 128, 128)], sems.at[j]
        )
        copy.start()
        leaving.append(copy)
        high, rest = halves(weight[:, part].astype(F32) * tiled)
        fold = ones_where((128, 256), lambda i: group(i) + 4 * j, channel)
        repeated = repeated + mm(high, fold) + mm(rest, fold)
    scatter_planes(repeated, across, out, 5)
    total = jnp.sum(messages[pl.ds(4, 128, stride=5), :], axis=0, keepdims=True)
    out[pl.ds(4, 128, stride=5), :] = jnp.broadcast_to(total, (128, 128))
    for copy in leaving:
        copy.wait()


def gelu_slope(preact):
    factor = math.sqrt(2.0 / math.pi)
    square = preact * preact
    tanh_value = jnp.tanh(preact * (factor + (factor * gelu_cubic) * square))
    rest = preact * (0.5 * factor + (1.5 * factor * gelu_cubic) * square)
    return 0.5 + 0.5 * tanh_value + rest * (1.0 - tanh_value * tanh_value)


def middle_kernel(
    own_in, other_in, bias, bypass, field_in, kept_in, depth_in, modes_in, cells_in,
    own, other, dpre_out,
    field, kept, dpre, depth, down_modes, down_cells, wide, high_in, rest_in, high, rest,
    stack, mixing, preact_even, preact_odd, flat, sums, bias_sums, in_sems, out_sems,
):
    small = [(modes_in, down_modes), (depth_in, depth), (cells_in, down_cells)]
    pairs = [pair for both in zip(block_pairs(field_in, field), block_pairs(kept_in, kept)) for pair in both]
    copies = start_copies(small + pairs, in_sems)
    leaving = [
        pltpu.make_async_copy(source, target, out_sems.at[i])
        for i, (source, target) in enumerate(block_pairs(dpre, dpre_out))
    ]
    mixing[...] = jnp.transpose(block_mixing(bypass)).astype(BF16)
    sums[...] = jnp.zeros_like(sums)
    bias_sums[...] = jnp.zeros_like(bias_sums)
    copies[0].wait()
    build_spread(down_modes, wide, high_in, rest_in)
    fill_inverse(own_in, other_in, 4, high_in, rest_in, stack)
    first = bias[...]
    bias_high, bias_left = halves(first)
    bias_rest, bias_last = halves(first - bias_high.astype(F32))
    lines = jnp.concatenate([bias_high, bias_rest, bias_last], axis=0).astype(F32)
    lines = jnp.concatenate([lines, jnp.zeros((13, C), F32)], axis=0).astype(BF16)
    wide_bias = mm(lines, ones_where((C, 32 * C), lambda i: i, channel)).astype(BF16)
    for x in range(2):
        stack[x, 3 * KZT : 3 * KZT + 16, :] = wide_bias
    copies[1].wait()
    preacts = (preact_even, preact_odd)

    def linear(i):
        copies[3 + 2 * i].wait()
        spectral = mm_tn(stack[i // 4, :, block_rows(i % 4)], depth[...])
        preacts[i % 2][...] = spectral + mm(mixing[...], field[block_rows(i), :])

    def activate(i):
        copies[4 + 2 * i].wait()
        for chunk in range(ROWS // 16):
            rows = slice(i * ROWS + chunk * 16, i * ROWS + chunk * 16 + 16)
            slope = gelu_slope(preacts[i % 2][chunk * 16 : chunk * 16 + 16, :])
            dpre[rows, :] = (kept[rows, :].astype(F32) * slope * keep_scale).astype(BF16)
        leaving[i].start()

    def reduce(i):
        part = dpre[block_rows(i), :]
        flat[i // 4, i % 4] = mm_nt(depth[0:KZT, :], part)
        sums[...] += mm_nt(field[block_rows(i), :], part)
        bias_sums[...] += mm_nt(jnp.ones((16, LZT), BF16), part)

    linear(0)
    copies[2].wait()
    build_spread(down_cells, wide, high, rest)
    for i in range(8):
        if i < 7:
            linear(i + 1)
        activate(i)
        reduce(i)

    send_modes(times_spread(joined(flat), high, rest), own, other, 5)
    lane = lax.broadcasted_iota(jnp.int32, (C, ROWS), 1) >> 5
    picked = jnp.zeros((C, ROWS), F32)
    for k in range(8):
        picked = jnp.where(lane == k, sums[k * C : (k + 1) * C, :], picked)
    both = jnp.concatenate([picked, bias_sums[...], jnp.zeros((16, ROWS), F32)], axis=0)
    fold = ones_where((ROWS, 128), channel, lambda i: i, F32)
    folded = jnp.dot(both, fold, precision=HIGHEST, preferred_element_type=F32)
    for side in range(2):
        own[pl.ds(side * 5 + 4, KZT, stride=10), :] = folded
        other[pl.ds(side * 5 + 4, KZT, stride=10), :] = jnp.zeros((KZT, 128), F32)
    for copy in leaving:
        copy.wait()


def last_kernel(
    own_in, other_in, bypass, dpre_in, depth_in, modes_in,
    grad_out, grad_weight, grad_bias,
    dpre, grad, depth, down_modes, wide, high_in, rest_in, stack, mixing, in_sems, out_sems,
):
    copies = start_copies([(modes_in, down_modes), (depth_in.at[pl.ds(0, 3 * KZT)], depth)] + block_pairs(dpre_in, dpre), in_sems)
    leaving = [
        pltpu.make_async_copy(source, target, out_sems.at[i])
        for i, (source, target) in enumerate(block_pairs(grad, grad_out))
    ]
    mixing[...] = block_mixing(bypass).astype(BF16)
    copies[0].wait()
    build_spread(down_modes, wide, high_in, rest_in)
    fill_inverse(own_in, other_in, 5, high_in, rest_in, stack)
    copies[1].wait()
    for i in range(8):
        copies[2 + i].wait()
        spectral = mm_tn(stack[i // 4, :, block_rows(i % 4)], depth[...])
        grad[block_rows(i), :] = (spectral + mm(mixing[...], dpre[block_rows(i), :])).astype(BF16)
        leaving[i].start()
    total = own_in[pl.ds(4, KZT, stride=10), :] + other_in[pl.ds(4, KZT, stride=10), :]
    total = total * norm_scale
    grad_weight[...] = total[0:C, 0:C]
    grad_bias[...] = total[C : C + 8, 0:C]
    for copy in leaving:
        copy.wait()


HELD = pl.BlockSpec(memory_space=pltpu.VMEM)
FAR = pl.BlockSpec(memory_space=pltpu.HBM)
SMEM = pl.BlockSpec(memory_space=pltpu.SMEM)
PARAMS = pltpu.CompilerParams(vmem_limit_bytes=24 * 1024 * 1024)


def like(*shape, dtype=F32):
    return jax.ShapeDtypeStruct(shape, dtype)


def call(kernel, name, ins, outs, out_shape, scratch=(), cost=None):
    return pl.pallas_call(
        kernel,
        name=name,
        in_specs=ins,
        out_specs=outs,
        out_shape=out_shape,
        scratch_shapes=list(scratch),
        compiler_params=PARAMS,
        cost_estimate=cost,
    )


def swap_cores(value):
    return lax.ppermute(value, "gy", [(i, i ^ 1) for i in range(GY)])


def exchange(messages, lines):
    groups = [[(g * 2 + side) * 2 + core for g in range(GX) for side in range(2)] for core in range(2)]
    shaped = messages.reshape(128, 1, lines * 128)
    moved = lax.all_to_all(
        shaped, ("gx", "gy"), split_axis=0, concat_axis=0, tiled=True, axis_index_groups=groups
    )
    return moved.reshape(128 * lines, 128)


def far(value):
    return pltpu.with_memory_space_constraint(value, pltpu.HBM)


def local(layer_input, cotangent, spectral_weight, bypass_weight, channel_bias, hash_key):
    table = {name: jnp.asarray(value) for name, value in tables().items()}
    across = table["across"]
    depth, down_cells, down_modes = (far(table[name]) for name in ("depth", "down_cells", "down_modes"))
    weight = spectral_weight.reshape(ROWS, C * C)
    field = far(layer_input.reshape(-1, LZT))
    field_far = pltpu.HBM((2048, LZT), BF16)
    held = lambda *shape, dtype=BF16: pltpu.VMEM(shape, dtype)
    sems = lambda count: pltpu.SemaphoreType.DMA((count,))
    field_held = held(2048, LZT)
    square = held(1024, 1024)
    flat = held(2, 4, KZT, ROWS, dtype=F32)
    stack = held(2, 3 * KZT + 16, 1024)
    last_stack = held(2, 3 * KZT, 1024)
    mixing = held(ROWS, ROWS)
    down = held(GY, 64, 32)
    wide = held(64, 1024, dtype=F32)
    depth_held = held(3 * KZT + 16, LZT)

    own, other = call(
        forward_kernel,
        "forward",
        [FAR] * 3,
        [HELD] * 2,
        [like(512, 128)] * 2,
        [field_held, held(KZT, LZT), down, wide, square, square, flat, sems(10)],
    )(field, depth, down_cells)
    messages = exchange(own + swap_cores(other), 4)

    kept = call(
        prepare_kernel,
        "prepare",
        [SMEM, FAR],
        FAR,
        field_far,
        [field_held, field_held, sems(8), sems(8)],
        pl.CostEstimate(flops=10**10, bytes_accessed=2 * 10**7, transcendentals=0),
    )(hash_key, far(cotangent.reshape(-1, LZT)))
    messages, kept = lax.optimization_barrier((messages, kept))

    planes, modes = call(mix_kernel, "mix", [HELD] * 3, [HELD] * 2, [like(512, 128), like(KX, ROWS)])(
        messages, weight, across
    )
    own_cells = exchange(planes, 4)
    other_cells = swap_cores(own_cells)

    preact = held(ROWS, LZT, dtype=F32)
    own, other, dpre = call(
        middle_kernel,
        "middle",
        [HELD] * 4 + [FAR] * 5,
        [HELD, HELD, FAR],
        [like(640, 128), like(640, 128), field_far],
        [
            field_held, field_held, field_held, depth_held, down, down, wide, square, square, square, square,
            stack, mixing, preact, preact, flat, held(ROWS, ROWS, dtype=F32), held(16, ROWS, dtype=F32),
            sems(19), sems(8),
        ],
    )(
        own_cells, other_cells, channel_bias.reshape(1, C), bypass_weight, field, far(kept), depth,
        down_modes, down_cells,
    )
    messages = exchange(own + swap_cores(other), 5)

    planes, grad_spectral = call(
        back_kernel,
        "back",
        [HELD] * 4,
        [HELD, FAR],
        [like(640, 128), pltpu.HBM((ROWS, 1024), F32)],
        [held(ROWS, 1024, dtype=F32), sems(8)],
    )(messages, modes, weight, across)
    own_cells = exchange(planes, 5)
    other_cells = swap_cores(own_cells)

    grad_input, grad_weight, grad_bias = call(
        last_kernel,
        "last",
        [HELD] * 3 + [FAR] * 3,
        [FAR, HELD, HELD],
        [field_far, like(C, C), like(8, C)],
        [
            field_held, field_held, held(3 * KZT, LZT), down, wide, square, square, last_stack, mixing,
            sems(10), sems(8),
        ],
    )(own_cells, other_cells, bypass_weight, far(dpre), depth, down_modes)
    return (
        grad_input.reshape(layer_input.shape),
        grad_spectral.reshape(spectral_weight.shape),
        grad_weight,
        grad_bias[0],
    )


def solution(mesh):
    return jax.shard_map(
        local,
        mesh=mesh,
        in_specs=(
            P("gx", "gy", None, None),
            P("gx", "gy", None, None),
            P("gy", "gx", None, None),
            P(),
            P(),
            P(),
        ),
        out_specs=(P("gx", "gy", None, None), P("gy", "gx", None, None), P(), P()),
        check_vma=False,
    )
```

```python
import math

import jax
import jax.numpy as jnp
import numpy as np
from jax import lax
from jax.experimental import pallas as pl
from jax.experimental.pallas import tpu as pltpu
from jax.sharding import PartitionSpec as P

LX = 128
LY = 128
LZ = 64
LT = 8
KX = 32
KY = 32
KZ = 16
KT = 4
C = 32
LZT = 512
KZT = 64
GX = 64
GY = 4
ROWS = 256
F32 = jnp.float32
BF16 = jnp.bfloat16
HIGHEST = lax.Precision.HIGHEST

keep_level = 6554
keep_scale = 1.0 / 0.9
gelu_cubic = 0.044715
mixer_one = -1640531535
mixer_two = -2048144789
mixer_three = -1028477387
norm_scale = 1.0 / math.sqrt(LX * LY * LZT)


def hartley_table(kept, length):
    wanted = np.arange(kept)
    frequency = np.where(wanted < kept // 2, wanted, wanted + (length - kept))
    residue = frequency[:, None] * np.arange(length)[None, :] % length
    radians = residue * (2.0 * math.pi / length)
    return ((np.cos(radians) + np.sin(radians)) / math.sqrt(length)).astype(np.float32)


def depth_table():
    joined = hartley_table(KZ, LZ)[:, None, :, None] * hartley_table(KT, LT)[None, :, None, :]
    return joined.reshape(KZT, LZT)


def split_table(table):
    high = table.astype(jnp.bfloat16)
    return high, (table - high.astype(np.float32)).astype(jnp.bfloat16)


def down_by_device():
    down = hartley_table(KY, LY)
    picked = []
    for q in range(GY):
        order = [
            ((side * 2 + (q % 2 + swap) % 2) * 8 + k)
            for swap in range(2)
            for side in range(2)
            for k in range(8)
        ]
        picked.append(down[order][:, q * 32 : (q + 1) * 32])
    return np.stack(picked)


def tables():
    down = down_by_device()
    low = lambda t: t.astype(jnp.bfloat16)
    depth = depth_table()
    depth_high, depth_rest = split_table(depth)
    across = hartley_table(KX, LX)
    gather = np.concatenate([np.repeat(across[:, x::2], 2, axis=1) for x in range(2)], axis=1)
    scatter = np.concatenate([across[:, x::2] for x in range(2)], axis=1)
    ones = np.concatenate([np.ones((3, LZT)), np.zeros((13, LZT))]).astype(jnp.bfloat16)
    return dict(
        down_cells=low(down.transpose(0, 2, 1)),
        down_modes=low(down),
        depth=np.concatenate([depth_high, depth_high, depth_rest, ones], axis=0),
        across=np.concatenate([gather, scatter], axis=1),
    )


def halves(value):
    high = value.astype(BF16)
    return high, (value - high.astype(F32)).astype(BF16)


def mm(a, b):
    return jnp.dot(a, b, preferred_element_type=F32)


def mm_nt(a, b):
    return lax.dot_general(a, b, (((1,), (1,)), ((), ())), preferred_element_type=F32)


def mm_tn(a, b):
    return lax.dot_general(a, b, (((0,), (0,)), ((), ())), preferred_element_type=F32)


def same(shape, rows, columns):
    row_ids = lax.broadcasted_iota(jnp.int32, shape, 0)
    column_ids = lax.broadcasted_iota(jnp.int32, shape, 1)
    return rows(row_ids) == columns(column_ids)


def ones_where(shape, rows, columns, dtype=BF16):
    return jnp.where(same(shape, rows, columns), 1.0, 0.0).astype(dtype)


def channel(index):
    return index & (C - 1)


def group(index):
    return index >> 5


def widen(table_ref):
    return mm(table_ref[lax.axis_index("gy")], ones_where((C, 32 * C), lambda i: i, group))


def fill_spread(wide_ref, columns, target_ref, first=0, count=32):
    mask = same((C, columns.stop - columns.start), lambda i: i, channel)
    for row in range(count):
        line = wide_ref[first + row : first + row + 1, columns]
        target_ref[row * C : (row + 1) * C, :] = jnp.where(mask, line, 0.0).astype(BF16)


OWN = slice(0, 512)
OTHER = slice(512, 1024)
ALL = slice(0, 1024)


def start_copies(pairs, sems):
    copies = [pltpu.make_async_copy(source, target, sems.at[i]) for i, (source, target) in enumerate(pairs)]
    for copy in copies:
        copy.start()
    return copies


def send_modes(modes, ref, lines):
    for side in range(2):
        for x in range(2):
            for half in range(2):
                at = (side * 2 + half) * 128
                ref[pl.ds(side * lines + x * 2 + half, KZT, stride=2 * lines), :] = modes[
                    x * KZT : (x + 1) * KZT, at : at + 128
                ]


def received_modes(ref, lines):
    rows = []
    for x in range(2):
        parts = [
            ref[pl.ds(side * lines + x * 2 + half, KZT, stride=2 * lines), :]
            for side in range(2)
            for half in range(2)
        ]
        rows.append(jnp.concatenate(parts, axis=1))
    return jnp.concatenate(rows, axis=0)


def block_mixing(weight_ref):
    weight = weight_ref[...].astype(F32)
    wide = jnp.concatenate([weight] * 8, axis=1)
    full = jnp.concatenate([wide] * 8, axis=0)
    return jnp.where(same((ROWS, ROWS), group, group), full, 0.0)


def fill_stack(cells, stack_ref):
    high, rest = halves(cells)
    for x in range(2):
        part = slice(x * KZT, (x + 1) * KZT)
        stack_ref[x, 0:KZT, :] = high[part]
        stack_ref[x, KZT : 2 * KZT, :] = rest[part]
        stack_ref[x, 2 * KZT : 3 * KZT, :] = high[part]


def block_rows(i):
    return slice(i * ROWS, (i + 1) * ROWS)


def block_pairs(source, target):
    return [(source.at[pl.ds(i * ROWS, ROWS)], target.at[pl.ds(i * ROWS, ROWS)]) for i in range(8)]


def forward_kernel(field_in, depth_in, down_in, other, cells, wide, field, depth, down, spread, flat, sems):
    copies = start_copies(
        [(down_in, down), (depth_in.at[pl.ds(0, KZT)], depth)] + block_pairs(field_in, field), sems
    )
    copies[0].wait()
    wide[...] = widen(down)
    fill_spread(wide, OTHER, spread)
    copies[1].wait()
    for first in (0, 4):
        for i in range(first, first + 4):
            copies[2 + i].wait()
        for i in range(first, first + 4):
            flat[i // 4, i % 4] = mm_nt(depth[...], field[block_rows(i), :])
    cells[...] = joined(flat).astype(BF16)
    send_modes(mm(cells[...], spread[...]), other, 4)


def forward_own_kernel(cells, wide, own, spread):
    fill_spread(wide, OWN, spread)
    send_modes(mm(cells[...], spread[...]), own, 4)


def joined(flat):
    return jnp.concatenate(
        [jnp.concatenate([flat[x, block] for block in range(4)], axis=1) for x in range(2)], axis=0
    )


def scramble(hashed):
    hashed = jnp.bitwise_xor(hashed, lax.shift_right_logical(hashed, jnp.int32(16)))
    hashed = hashed * jnp.int32(mixer_two)
    hashed = jnp.bitwise_xor(hashed, lax.shift_right_logical(hashed, jnp.int32(13)))
    hashed = hashed * jnp.int32(mixer_three)
    return jnp.bitwise_xor(hashed, lax.shift_right_logical(hashed, jnp.int32(16)))


def prepare_kernel(key, cotangent_in, kept_out, cotangent, kept, in_sems, out_sems):
    arriving = start_copies(block_pairs(cotangent_in, cotangent), in_sems)
    leaving = [pltpu.make_async_copy(source, target, out_sems.at[i]) for i, (source, target) in enumerate(block_pairs(kept, kept_out))]
    origin = (lax.axis_index("gx") * 2 * LY + lax.axis_index("gy") * 32) * (C * LZT)
    shape = (16, LZT)
    inside = (
        lax.broadcasted_iota(jnp.int32, shape, 0) * LZT + lax.broadcasted_iota(jnp.int32, shape, 1)
    ) * jnp.int32(mixer_one)
    for i in range(8):
        first = origin + ((i // 4) * LY + (i % 4) * 8) * (C * LZT)
        arriving[i].wait()

        def body(chunk, carry):
            for part in range(4):
                at = chunk * 64 + part * 16
                start = (first + at * LZT) * jnp.int32(mixer_one) + key[0]
                hashed = scramble(inside + start)
                hashed = scramble(jnp.bitwise_xor(hashed, key[1]))
                keep = jnp.bitwise_and(hashed, jnp.int32(65535)) >= keep_level
                rows = pl.ds(pl.multiple_of(i * ROWS + at, 16), 16)
                kept[rows, :] = jnp.where(keep, cotangent[rows, :].astype(F32), 0.0).astype(BF16)
            return carry

        lax.fori_loop(0, 4, body, 0)
        leaving[i].start()
    for copy in leaving:
        copy.wait()


def gathered_modes(messages, across, lines):
    slabs = [
        jnp.concatenate([messages[pl.ds(x * 2 + half, 128, stride=lines), :] for half in range(2)], axis=1)
        for x in range(2)
    ]
    slabs = jnp.concatenate(slabs, axis=0)
    return jnp.dot(across[:, 0:256], slabs, precision=HIGHEST, preferred_element_type=F32)


def by_mode(modes):
    return jnp.concatenate([modes[:, k * C : (k + 1) * C] for k in range(8)], axis=0)


def wide_halves(value):
    return jnp.concatenate(halves(value), axis=1)


def scatter_planes(repeated, across, out, lines):
    lane = lax.broadcasted_iota(jnp.int32, (KX, ROWS), 1) >> 5
    modes = jnp.zeros((KX, ROWS), F32)
    for k in range(8):
        modes = jnp.where(lane == k, repeated[k * KX : (k + 1) * KX, :], modes)
    planes = lax.dot_general(
        across[:, 256:384], modes, (((0,), (0,)), ((), ())), precision=HIGHEST, preferred_element_type=F32
    )
    for x in range(2):
        for half in range(2):
            piece = planes[x * GX : (x + 1) * GX, half * 128 : (half + 1) * 128]
            for side in range(2):
                out[pl.ds(side * lines + x * 2 + half, GX, stride=2 * lines), :] = piece


def mix_kernel(messages, weight, across, out, modes_out):
    modes = gathered_modes(messages, across, 4)
    modes_out[...] = modes
    spread = mm(wide_halves(by_mode(modes)), ones_where((2 * C, C * C), channel, group))
    total = jnp.zeros((ROWS, 128), F32)
    for j in range(8):
        part = slice(j * 128, (j + 1) * 128)
        total = total + spread[:, part] * weight[:, part].astype(F32)
    repeated = mm(wide_halves(total), ones_where((256, 256), channel, channel))
    scatter_planes(repeated, across, out, 4)


def back_kernel(messages, weight, across, out, dmodes_out):
    dmodes = gathered_modes(messages, across, 5)
    dmodes_out[...] = dmodes
    tiled = mm(wide_halves(by_mode(dmodes)), ones_where((2 * C, 128), channel, channel))
    repeated = jnp.zeros((ROWS, ROWS), F32)
    for j in range(8):
        high, rest = halves(weight[:, j * 128 : (j + 1) * 128].astype(F32) * tiled)
        fold = ones_where((128, 256), lambda i: group(i) + 4 * j, channel)
        repeated = repeated + mm(high, fold) + mm(rest, fold)
    scatter_planes(repeated, across, out, 5)
    total = jnp.sum(messages[pl.ds(4, 128, stride=5), :], axis=0, keepdims=True)
    out[pl.ds(4, 128, stride=5), :] = jnp.broadcast_to(total, (128, 128))


def gelu_slope(preact):
    factor = math.sqrt(2.0 / math.pi)
    square = preact * preact
    tanh_value = jnp.tanh(preact * (factor + (factor * gelu_cubic) * square))
    rest = preact * (0.5 * factor + (1.5 * factor * gelu_cubic) * square)
    return 0.5 + 0.5 * tanh_value + rest * (1.0 - tanh_value * tanh_value)


def invert_own(own_in, lines, down_modes, part, spread_other, wide, spread):
    wide[...] = widen(down_modes)
    fill_spread(wide, ALL, spread, 0, 16)
    part[...] = mm(received_modes(own_in, lines).astype(BF16), spread[...])
    fill_spread(wide, ALL, spread_other, 16, 16)


def middle_own_kernel(
    own_in, field_in, kept_in, depth_in, modes_in, cells_in,
    part, spread_other, spread_cells, field, kept, depth,
    down_modes, down_cells, wide, wide_cells, spread, sems,
):
    copies = start_copies(
        [(modes_in, down_modes), (cells_in, down_cells), (depth_in, depth)]
        + block_pairs(field_in, field)
        + block_pairs(kept_in, kept),
        sems,
    )
    copies[0].wait()
    copies[1].wait()
    invert_own(own_in, 4, down_modes, part, spread_other, wide, spread)
    wide_cells[...] = widen(down_cells)
    fill_spread(wide_cells, ALL, spread_cells)
    for copy in copies[2:]:
        copy.wait()


def middle_kernel(
    other_in, part, spread_other, spread_cells, field, kept, depth, bias, bypass,
    other, cells, sums, bias_sums, dpre_out,
    dpre_even, dpre_odd, stack, mixing, preact_even, preact_odd, flat, sems,
):
    mixing[...] = jnp.transpose(block_mixing(bypass)).astype(BF16)
    sums[...] = jnp.zeros_like(sums)
    bias_sums[...] = jnp.zeros_like(bias_sums)
    inverted = part[...] + mm(received_modes(other_in, 4).astype(BF16), spread_other[...])
    fill_stack(inverted, stack)
    first = bias[...]
    bias_high = first.astype(BF16)
    bias_rest, bias_last = halves(first - bias_high.astype(F32))
    lines = jnp.concatenate([bias_high, bias_rest, bias_last], axis=0).astype(F32)
    lines = jnp.concatenate([lines, jnp.zeros((13, C), F32)], axis=0).astype(BF16)
    wide_bias = mm(lines, ones_where((C, 32 * C), lambda i: i, channel)).astype(BF16)
    for x in range(2):
        stack[x, 3 * KZT : 3 * KZT + 16, :] = wide_bias
    preacts = (preact_even, preact_odd)
    dpres = (dpre_even, dpre_odd)

    def leaving(i):
        rows = pl.ds((i // 2) * ROWS, ROWS)
        return pltpu.make_async_copy(dpres[i % 2].at[rows], dpre_out.at[pl.ds(i * ROWS, ROWS)], sems.at[i])

    def held_rows(i):
        return slice((i // 2) * ROWS, (i // 2 + 1) * ROWS)

    def linear(i):
        spectral = mm_tn(stack[i // 4, :, block_rows(i % 4)], depth[...])
        preacts[i % 2][...] = spectral + mm(mixing[...], field[block_rows(i), :])

    def activate(i):
        for chunk in range(ROWS // 16):
            rows = slice(i * ROWS + chunk * 16, i * ROWS + chunk * 16 + 16)
            at = (i // 2) * ROWS + chunk * 16
            slope = gelu_slope(preacts[i % 2][chunk * 16 : chunk * 16 + 16, :])
            dpres[i % 2][at : at + 16, :] = (kept[rows, :].astype(F32) * slope * keep_scale).astype(BF16)

    def reduce(i):
        block = dpres[i % 2][held_rows(i), :]
        flat[i // 4, i % 4] = mm_nt(depth[0:KZT, :], block)
        sums[...] += mm_nt(field[block_rows(i), :], block)
        bias_sums[...] += mm_nt(jnp.ones((16, LZT), BF16), block)

    linear(0)
    for i in range(9):
        if i > 0:
            leaving(i - 1).start()
        if i < 7:
            linear(i + 1)
        if i > 0:
            reduce(i - 1)
        if i < 8:
            activate(i)

    cells[...] = joined(flat).astype(BF16)
    send_modes(mm(cells[...], spread_cells[:, OTHER]), other, 5)
    for side in range(2):
        other[pl.ds(side * 5 + 4, KZT, stride=10), :] = jnp.zeros((KZT, 128), F32)
    for i in range(8):
        leaving(i).wait()


def middle_send_kernel(cells, spread_cells, sums, bias_sums, own):
    send_modes(mm(cells[...], spread_cells[:, OWN]), own, 5)
    lane = lax.broadcasted_iota(jnp.int32, (C, ROWS), 1) >> 5
    picked = jnp.zeros((C, ROWS), F32)
    for k in range(8):
        picked = jnp.where(lane == k, sums[k * C : (k + 1) * C, :], picked)
    both = jnp.concatenate([picked, bias_sums[...], jnp.zeros((16, ROWS), F32)], axis=0)
    fold = ones_where((ROWS, 128), channel, lambda i: i, F32)
    folded = jnp.dot(both, fold, precision=HIGHEST, preferred_element_type=F32)
    for side in range(2):
        own[pl.ds(side * 5 + 4, KZT, stride=10), :] = folded


def last_own_kernel(
    own_in, modes, dmodes, dpre_in, depth_in, modes_in,
    part, spread_other, dpre, depth, grad_out,
    down_modes, wide, spread, grad, sems, out_sems,
):
    copies = start_copies(
        [(modes_in, down_modes), (depth_in.at[pl.ds(0, 3 * KZT)], depth)] + block_pairs(dpre_in, dpre), sems
    )
    tiled = mm(wide_halves(by_mode(dmodes[...])), ones_where((2 * C, 128), channel, channel))
    expanded = mm(wide_halves(by_mode(modes[...])), ones_where((2 * C, C * C), channel, group))
    for j in range(8):
        grad[:, j * 128 : (j + 1) * 128] = expanded[:, j * 128 : (j + 1) * 128] * tiled
    leaving = pltpu.make_async_copy(grad, grad_out, out_sems.at[0])
    leaving.start()
    copies[0].wait()
    invert_own(own_in, 5, down_modes, part, spread_other, wide, spread)
    for copy in copies[1:]:
        copy.wait()
    leaving.wait()


def last_kernel(
    own_in, other_in, part, spread_other, dpre, depth, bypass,
    grad_out, grad_weight, grad_bias,
    grad, stack, mixing, sems,
):
    mixing[...] = block_mixing(bypass).astype(BF16)
    inverted = part[...] + mm(received_modes(other_in, 5).astype(BF16), spread_other[...])
    fill_stack(inverted, stack)
    total = own_in[pl.ds(4, KZT, stride=10), :] + other_in[pl.ds(4, KZT, stride=10), :]
    total = total * norm_scale
    grad_weight[...] = total[0:C, 0:C]
    grad_bias[...] = total[C : C + 1, 0:C]
    copies = [
        pltpu.make_async_copy(source, target, sems.at[i])
        for i, (source, target) in enumerate(block_pairs(grad, grad_out))
    ]
    for first in range(0, 8, 2):
        for i in (first, first + 1):
            spectral = mm_tn(stack[i // 4, :, block_rows(i % 4)], depth[...])
            grad[block_rows(i), :] = (spectral + mm(mixing[...], dpre[block_rows(i), :])).astype(BF16)
        copies[first].start()
        copies[first + 1].start()
    for copy in copies:
        copy.wait()


HELD = pl.BlockSpec(memory_space=pltpu.VMEM)
FAR = pl.BlockSpec(memory_space=pltpu.HBM)
SMEM = pl.BlockSpec(memory_space=pltpu.SMEM)
PARAMS = pltpu.CompilerParams(vmem_limit_bytes=24 * 1024 * 1024)


SHORT = pl.CostEstimate(flops=2 * 10**9, bytes_accessed=4 * 10**6, transcendentals=0)
LONG = pl.CostEstimate(flops=10**10, bytes_accessed=2 * 10**7, transcendentals=0)


def like(*shape, dtype=F32):
    return jax.ShapeDtypeStruct(shape, dtype)


def call(kernel, name, ins, outs, out_shape, scratch=(), cost=None):
    return pl.pallas_call(
        kernel,
        name=name,
        in_specs=ins,
        out_specs=outs,
        out_shape=out_shape,
        scratch_shapes=list(scratch),
        compiler_params=PARAMS,
        cost_estimate=cost,
    )


def swap_cores(value):
    return lax.ppermute(value, "gy", [(i, i ^ 1) for i in range(GY)])


def exchange(messages, lines):
    groups = [[(g * 2 + side) * 2 + core for g in range(GX) for side in range(2)] for core in range(2)]
    shaped = messages.reshape(128, 1, lines * 128)
    moved = lax.all_to_all(
        shaped, ("gx", "gy"), split_axis=0, concat_axis=0, tiled=True, axis_index_groups=groups
    )
    return moved.reshape(128 * lines, 128)


def far(value):
    return pltpu.with_memory_space_constraint(value, pltpu.HBM)


def local(layer_input, cotangent, spectral_weight, bypass_weight, channel_bias, hash_key):
    table = {name: jnp.asarray(value) for name, value in tables().items()}
    across = table["across"]
    depth, down_cells, down_modes = (far(table[name]) for name in ("depth", "down_cells", "down_modes"))
    weight = spectral_weight.reshape(ROWS, C * C)
    field = far(layer_input.reshape(-1, LZT))
    field_far = pltpu.HBM((2048, LZT), BF16)
    held = lambda *shape, dtype=BF16: pltpu.VMEM(shape, dtype)
    sems = lambda count: pltpu.SemaphoreType.DMA((count,))
    field_held = held(2048, LZT)
    flat = held(2, 4, KZT, ROWS, dtype=F32)
    mixing = held(ROWS, ROWS)
    down = held(GY, 32, 32)
    wide = held(32, 1024, dtype=F32)
    half_rows = held(512, 1024)
    half_columns = held(1024, 512)
    part_like = like(128, 1024)
    cells_like = like(128, 1024, dtype=BF16)
    spread_like = like(512, 1024, dtype=BF16)
    field_like = like(2048, LZT, dtype=BF16)

    other, cells, wide_cells = call(
        forward_kernel,
        "forward",
        [FAR] * 3,
        [HELD] * 3,
        [like(512, 128), cells_like, like(32, 1024)],
        [field_held, held(KZT, LZT), down, half_columns, flat, sems(10)],
    )(field, depth, down_cells)
    arriving = swap_cores(other)
    own = call(forward_own_kernel, "forward_own", [HELD] * 2, HELD, like(512, 128), [half_columns], cost=SHORT)(
        cells, wide_cells
    )
    messages = exchange(own + arriving, 4)

    kept = call(
        prepare_kernel, "prepare", [SMEM, FAR], FAR, field_far, [field_held, field_held, sems(8), sems(8)], cost=LONG
    )(hash_key, far(cotangent.reshape(-1, LZT)))
    messages, kept = lax.optimization_barrier((messages, kept))

    planes, modes = call(mix_kernel, "mix", [HELD] * 3, [HELD] * 2, [like(512, 128), like(KX, ROWS)])(
        messages, weight, across
    )
    own_cells = exchange(planes, 4)
    other_cells = swap_cores(own_cells)
    part, spread_other, spread_cells, field_near, kept_near, depth_near = call(
        middle_own_kernel,
        "middle_own",
        [HELD] + [FAR] * 5,
        [HELD] * 6,
        [
            part_like, spread_like, like(1024, 1024, dtype=BF16), field_like, field_like,
            like(3 * KZT + 16, LZT, dtype=BF16),
        ],
        [down, down, wide, wide, half_rows, sems(19)],
        SHORT,
    )(own_cells, field, far(kept), depth, down_modes, down_cells)

    preact = held(ROWS, LZT, dtype=F32)
    half_field = held(1024, LZT)
    other, cells, sums, bias_sums, dpre = call(
        middle_kernel,
        "middle",
        [HELD] * 9,
        [HELD] * 4 + [FAR],
        [like(640, 128), cells_like, like(ROWS, ROWS), like(16, ROWS), field_far],
        [half_field, half_field, held(2, 3 * KZT + 16, 1024), mixing, preact, preact, flat, sems(8)],
    )(
        other_cells, part, spread_other, spread_cells, field_near, kept_near, depth_near,
        channel_bias.reshape(1, C), bypass_weight,
    )
    arriving = swap_cores(other)
    own = call(middle_send_kernel, "middle_send", [HELD] * 4, HELD, like(640, 128), cost=SHORT)(
        cells, spread_cells, sums, bias_sums
    )
    messages = exchange(own + arriving, 5)

    planes, dmodes = call(back_kernel, "back", [HELD] * 3, [HELD] * 2, [like(640, 128), like(KX, ROWS)])(
        messages, weight, across
    )
    own_cells = exchange(planes, 5)
    other_cells = swap_cores(own_cells)
    part, spread_other, dpre_near, depth_near, grad_spectral = call(
        last_own_kernel,
        "last_own",
        [HELD] * 3 + [FAR] * 3,
        [HELD] * 4 + [FAR],
        [part_like, spread_like, field_like, like(3 * KZT, LZT, dtype=BF16), pltpu.HBM((ROWS, 1024), F32)],
        [down, wide, half_rows, held(ROWS, 1024, dtype=F32), sems(10), sems(1)],
        SHORT,
    )(own_cells, modes, dmodes, far(dpre), depth, down_modes)

    grad_input, grad_weight, grad_bias = call(
        last_kernel,
        "last",
        [HELD] * 7,
        [FAR, HELD, HELD],
        [field_far, like(C, C), like(1, C)],
        [field_held, held(2, 3 * KZT, 1024), mixing, sems(8)],
    )(own_cells, other_cells, part, spread_other, dpre_near, depth_near, bypass_weight)
    return (
        grad_input.reshape(layer_input.shape),
        grad_spectral.reshape(spectral_weight.shape),
        grad_weight,
        grad_bias.reshape(C),
    )


def solution(mesh):
    return jax.shard_map(
        local,
        mesh=mesh,
        in_specs=(
            P("gx", "gy", None, None),
            P("gx", "gy", None, None),
            P("gy", "gx", None, None),
            P(),
            P(),
            P(),
        ),
        out_specs=(P("gx", "gy", None, None), P("gy", "gx", None, None), P(), P()),
        check_vma=False,
    )
```

```python
import math

import jax
import jax.numpy as jnp
import numpy as np
from jax import lax
from jax.experimental import pallas as pl
from jax.experimental.pallas import tpu as pltpu
from jax.sharding import PartitionSpec as P

LX = 128
LY = 128
LZ = 64
LT = 8
KX = 32
KY = 32
KZ = 16
KT = 4
C = 32
LZT = 512
KZT = 64
GX = 64
GY = 4
ROWS = 256
F32 = jnp.float32
BF16 = jnp.bfloat16
HIGHEST = lax.Precision.HIGHEST

keep_level = 6554
keep_scale = 1.0 / 0.9
gelu_cubic = 0.044715
mixer_one = -1640531535
mixer_two = -2048144789
mixer_three = -1028477387
norm_scale = 1.0 / math.sqrt(LX * LY * LZT)


def hartley_table(kept, length):
    wanted = np.arange(kept)
    frequency = np.where(wanted < kept // 2, wanted, wanted + (length - kept))
    residue = frequency[:, None] * np.arange(length)[None, :] % length
    radians = residue * (2.0 * math.pi / length)
    return ((np.cos(radians) + np.sin(radians)) / math.sqrt(length)).astype(np.float32)


def depth_table():
    joined = hartley_table(KZ, LZ)[:, None, :, None] * hartley_table(KT, LT)[None, :, None, :]
    return joined.reshape(KZT, LZT)


def split_table(table):
    high = table.astype(jnp.bfloat16)
    return high, (table - high.astype(np.float32)).astype(jnp.bfloat16)


def down_by_device():
    down = hartley_table(KY, LY)
    picked = []
    for q in range(GY):
        order = [
            ((side * 2 + (q % 2 + swap) % 2) * 8 + k)
            for swap in range(2)
            for side in range(2)
            for k in range(8)
        ]
        picked.append(down[order][:, q * 32 : (q + 1) * 32])
    return np.stack(picked)


def tables():
    down = down_by_device()
    low = lambda t: t.astype(jnp.bfloat16)
    depth = depth_table()
    depth_high, depth_rest = split_table(depth)
    across = hartley_table(KX, LX)
    gather = np.concatenate([np.repeat(across[:, x::2], 2, axis=1) for x in range(2)], axis=1)
    scatter = np.concatenate([across[:, x::2] for x in range(2)], axis=1)
    scatter_high, scatter_rest = split_table(scatter)
    scatter_stack = np.concatenate([scatter_high, scatter_high, scatter_rest], axis=0).T.copy()
    ones = np.concatenate([np.ones((3, LZT)), np.zeros((13, LZT))]).astype(jnp.bfloat16)
    return dict(
        down_cells=low(down.transpose(0, 2, 1)),
        down_modes=low(down),
        depth=np.concatenate([depth_high, depth_high, depth_rest, ones], axis=0),
        gather=np.concatenate(split_table(gather), axis=0),
        scatter=scatter_stack,
    )


def halves(value):
    high = value.astype(BF16)
    return high, (value - high.astype(F32)).astype(BF16)


def mm(a, b):
    return jnp.dot(a, b, preferred_element_type=F32)


def mm_nt(a, b):
    return lax.dot_general(a, b, (((1,), (1,)), ((), ())), preferred_element_type=F32)


def mm_tn(a, b):
    return lax.dot_general(a, b, (((0,), (0,)), ((), ())), preferred_element_type=F32)


def same(shape, rows, columns):
    row_ids = lax.broadcasted_iota(jnp.int32, shape, 0)
    column_ids = lax.broadcasted_iota(jnp.int32, shape, 1)
    return rows(row_ids) == columns(column_ids)


def ones_where(shape, rows, columns, dtype=BF16):
    return jnp.where(same(shape, rows, columns), 1.0, 0.0).astype(dtype)


def channel(index):
    return index & (C - 1)


def group(index):
    return index >> 5


def widen(table_ref):
    return mm(table_ref[lax.axis_index("gy")], ones_where((C, 32 * C), lambda i: i, group))


def fill_spread(wide_ref, columns, target_ref, first=0, count=32):
    mask = same((C, columns.stop - columns.start), lambda i: i, channel)
    for row in range(count):
        line = wide_ref[first + row : first + row + 1, columns]
        target_ref[row * C : (row + 1) * C, :] = jnp.where(mask, line, 0.0).astype(BF16)


OWN = slice(0, 512)
OTHER = slice(512, 1024)
ALL = slice(0, 1024)


def start_copies(pairs, sems):
    copies = [pltpu.make_async_copy(source, target, sems.at[i]) for i, (source, target) in enumerate(pairs)]
    for copy in copies:
        copy.start()
    return copies


def send_modes(modes, ref, lines):
    for side in range(2):
        for x in range(2):
            for half in range(2):
                at = (side * 2 + half) * 128
                ref[pl.ds(side * lines + x * 2 + half, KZT, stride=2 * lines), :] = modes[
                    x * KZT : (x + 1) * KZT, at : at + 128
                ]


def received_modes(ref, lines):
    rows = []
    for x in range(2):
        parts = [
            ref[pl.ds(side * lines + x * 2 + half, KZT, stride=2 * lines), :]
            for side in range(2)
            for half in range(2)
        ]
        rows.append(jnp.concatenate(parts, axis=1))
    return jnp.concatenate(rows, axis=0)


def block_mixing(weight_ref):
    weight = weight_ref[...].astype(F32)
    wide = jnp.concatenate([weight] * 8, axis=1)
    full = jnp.concatenate([wide] * 8, axis=0)
    return jnp.where(same((ROWS, ROWS), group, group), full, 0.0)


def fill_stack(cells, stack_ref):
    high, rest = halves(cells)
    for x in range(2):
        part = slice(x * KZT, (x + 1) * KZT)
        stack_ref[x, 0:KZT, :] = high[part]
        stack_ref[x, KZT : 2 * KZT, :] = rest[part]
        stack_ref[x, 2 * KZT : 3 * KZT, :] = high[part]


def block_rows(i):
    return slice(i * ROWS, (i + 1) * ROWS)


def block_pairs(source, target):
    return [(source.at[pl.ds(i * ROWS, ROWS)], target.at[pl.ds(i * ROWS, ROWS)]) for i in range(8)]


def forward_kernel(field_in, depth_in, down_in, other, cells, wide, field, depth, down, spread, flat, sems):
    copies = start_copies(
        [(down_in, down), (depth_in.at[pl.ds(0, KZT)], depth)] + block_pairs(field_in, field), sems
    )
    copies[0].wait()
    wide[...] = widen(down)
    fill_spread(wide, OTHER, spread)
    copies[1].wait()
    for first in (0, 2, 4, 6):
        for i in range(first, first + 2):
            copies[2 + i].wait()
        for i in range(first, first + 2):
            flat[i // 4, i % 4] = mm_nt(depth[...], field[block_rows(i), :])
    cells[...] = joined(flat).astype(BF16)
    send_modes(mm(cells[...], spread[...]), other, 4)


def forward_own_kernel(cells, wide, own, spread):
    fill_spread(wide, OWN, spread)
    send_modes(mm(cells[...], spread[...]), own, 4)


def joined(flat):
    return jnp.concatenate(
        [jnp.concatenate([flat[x, block] for block in range(4)], axis=1) for x in range(2)], axis=0
    )


def scramble(hashed):
    hashed = jnp.bitwise_xor(hashed, lax.shift_right_logical(hashed, jnp.int32(16)))
    hashed = hashed * jnp.int32(mixer_two)
    hashed = jnp.bitwise_xor(hashed, lax.shift_right_logical(hashed, jnp.int32(13)))
    hashed = hashed * jnp.int32(mixer_three)
    return jnp.bitwise_xor(hashed, lax.shift_right_logical(hashed, jnp.int32(16)))


def prepare_kernel(key, cotangent_in, kept, cotangent, in_sems):
    arriving = start_copies(block_pairs(cotangent_in, cotangent), in_sems)
    origin = (lax.axis_index("gx") * 2 * LY + lax.axis_index("gy") * 32) * (C * LZT)
    shape = (16, LZT)
    inside = (
        lax.broadcasted_iota(jnp.int32, shape, 0) * LZT + lax.broadcasted_iota(jnp.int32, shape, 1)
    ) * jnp.int32(mixer_one)
    for i in range(8):
        first = origin + ((i // 4) * LY + (i % 4) * 8) * (C * LZT)
        arriving[i].wait()

        def body(chunk, carry):
            for part in range(4):
                at = chunk * 64 + part * 16
                start = (first + at * LZT) * jnp.int32(mixer_one) + key[0]
                hashed = scramble(inside + start)
                hashed = scramble(jnp.bitwise_xor(hashed, key[1]))
                keep = jnp.bitwise_and(hashed, jnp.int32(65535)) >= keep_level
                rows = pl.ds(pl.multiple_of(i * ROWS + at, 16), 16)
                kept[rows, :] = jnp.where(keep, cotangent[rows, :].astype(F32), 0.0).astype(BF16)
            return carry

        lax.fori_loop(0, 4, body, 0)


def gathered_modes(messages, gather, lines):
    slabs = [
        jnp.concatenate([messages[pl.ds(x * 2 + half, 128, stride=lines), :] for half in range(2)], axis=1)
        for x in range(2)
    ]
    high, rest = halves(jnp.concatenate(slabs, axis=0))
    both = mm(gather[...], high)
    return both[0:KX] + both[KX : 2 * KX] + mm(gather[0:KX, :], rest)


def by_mode(modes):
    return jnp.concatenate([modes[:, k * C : (k + 1) * C] for k in range(8)], axis=0)


def wide_halves(value):
    return jnp.concatenate(halves(value), axis=1)


def scatter_planes(repeated, scatter, out, lines):
    lane = lax.broadcasted_iota(jnp.int32, (KX, ROWS), 1) >> 5
    modes = jnp.zeros((KX, ROWS), F32)
    for k in range(8):
        modes = jnp.where(lane == k, repeated[k * KX : (k + 1) * KX, :], modes)
    high, rest = halves(modes)
    planes = mm(scatter[...], jnp.concatenate([high, rest, high], axis=0))
    for x in range(2):
        for half in range(2):
            piece = planes[x * GX : (x + 1) * GX, half * 128 : (half + 1) * 128]
            for side in range(2):
                out[pl.ds(side * lines + x * 2 + half, GX, stride=2 * lines), :] = piece


def mix_kernel(messages, weight, gather, scatter, out, modes_out):
    modes = gathered_modes(messages, gather, 4)
    modes_out[...] = modes
    spread = mm(wide_halves(by_mode(modes)), ones_where((2 * C, C * C), channel, group))
    total = jnp.zeros((ROWS, 128), F32)
    for j in range(8):
        part = slice(j * 128, (j + 1) * 128)
        total = total + spread[:, part] * weight[:, part].astype(F32)
    repeated = mm(wide_halves(total), ones_where((256, 256), channel, channel))
    scatter_planes(repeated, scatter, out, 4)


def back_kernel(messages, weight, gather, scatter, out, dmodes_out):
    dmodes = gathered_modes(messages, gather, 5)
    dmodes_out[...] = dmodes
    tiled = mm(wide_halves(by_mode(dmodes)), ones_where((2 * C, 128), channel, channel))
    repeated = jnp.zeros((ROWS, ROWS), F32)
    for j in range(8):
        high, rest = halves(weight[:, j * 128 : (j + 1) * 128].astype(F32) * tiled)
        fold = ones_where((128, 256), lambda i: group(i) + 4 * j, channel)
        repeated = repeated + mm(high, fold) + mm(rest, fold)
    scatter_planes(repeated, scatter, out, 5)
    total = jnp.sum(messages[pl.ds(4, 128, stride=5), :], axis=0, keepdims=True)
    out[pl.ds(4, 128, stride=5), :] = jnp.broadcast_to(total, (128, 128))


def scaled_slope(preact):
    factor = math.sqrt(2.0 / math.pi)
    square = preact * preact
    tanh_value = jnp.tanh(preact * (factor + (factor * gelu_cubic) * square))
    half = 0.5 * keep_scale
    rest = preact * (half * factor + (half * 3.0 * factor * gelu_cubic) * square)
    return (1.0 + tanh_value) * (half + rest * (1.0 - tanh_value))


def invert_own(own_in, lines, down_modes, part, spread_other, wide, spread):
    wide[...] = widen(down_modes)
    fill_spread(wide, ALL, spread, 0, 16)
    part[...] = mm(received_modes(own_in, lines).astype(BF16), spread[...])
    fill_spread(wide, ALL, spread_other, 16, 16)


def middle_own_kernel(
    own_in, field_in, depth_in, modes_in, cells_in,
    part, spread_other, spread_cells, field, depth,
    down_modes, down_cells, wide, wide_cells, spread, sems,
):
    copies = start_copies(
        [(modes_in, down_modes), (cells_in, down_cells), (depth_in, depth)]
        + [(field_in.at[pl.ds(i * ROWS, ROWS)], field.at[i, pl.ds(KZT, ROWS)]) for i in range(8)],
        sems,
    )
    copies[0].wait()
    copies[1].wait()
    invert_own(own_in, 4, down_modes, part, spread_other, wide, spread)
    wide_cells[...] = widen(down_cells)
    fill_spread(wide_cells, ALL, spread_cells)
    copies[2].wait()
    for i in range(8):
        field[i, 0:KZT, :] = depth[0:KZT, :]
        field[i, KZT + ROWS :, :] = jnp.ones((16, LZT), BF16)
    for copy in copies[3:]:
        copy.wait()


def middle_kernel(
    other_in, part, spread_other, spread_cells, field, kept, depth, bias, bypass,
    other, cells, sums, bias_sums, dpre,
    stack, mixing, preact_even, preact_odd, flat,
):
    mixing[...] = jnp.transpose(block_mixing(bypass)).astype(BF16)
    sums[...] = jnp.zeros_like(sums)
    bias_sums[...] = jnp.zeros_like(bias_sums)
    inverted = part[...] + mm(received_modes(other_in, 4).astype(BF16), spread_other[...])
    fill_stack(inverted, stack)
    first = bias[...]
    bias_high = first.astype(BF16)
    bias_rest, bias_last = halves(first - bias_high.astype(F32))
    lines = jnp.concatenate([bias_high, bias_rest, bias_last], axis=0).astype(F32)
    lines = jnp.concatenate([lines, jnp.zeros((13, C), F32)], axis=0).astype(BF16)
    wide_bias = mm(lines, ones_where((C, 32 * C), lambda i: i, channel)).astype(BF16)
    for x in range(2):
        stack[x, 3 * KZT : 3 * KZT + 16, :] = wide_bias
    preacts = (preact_even, preact_odd)

    def linear(i):
        spectral = mm_tn(stack[i // 4, :, block_rows(i % 4)], depth[...])
        preacts[i % 2][...] = spectral + mm(mixing[...], field[i, KZT : KZT + ROWS, :])

    def activate(i):
        for chunk in range(ROWS // 16):
            rows = slice(i * ROWS + chunk * 16, i * ROWS + chunk * 16 + 16)
            slope = scaled_slope(preacts[i % 2][chunk * 16 : chunk * 16 + 16, :])
            dpre[rows, :] = (kept[rows, :].astype(F32) * slope).astype(BF16)

    def reduce(i):
        found = mm_nt(field[i], dpre[block_rows(i), :])
        flat[i // 4, i % 4] = found[0:KZT]
        sums[...] += found[KZT : KZT + ROWS]
        bias_sums[...] += found[KZT + ROWS :]

    linear(0)
    for i in range(9):
        if i < 7:
            linear(i + 1)
        if i > 0:
            reduce(i - 1)
        if i < 8:
            activate(i)

    cells[...] = joined(flat).astype(BF16)
    send_modes(mm(cells[...], spread_cells[:, OTHER]), other, 5)
    for side in range(2):
        other[pl.ds(side * 5 + 4, KZT, stride=10), :] = jnp.zeros((KZT, 128), F32)


def middle_send_kernel(cells, spread_cells, sums, bias_sums, own):
    send_modes(mm(cells[...], spread_cells[:, OWN]), own, 5)
    lane = lax.broadcasted_iota(jnp.int32, (C, ROWS), 1) >> 5
    picked = jnp.zeros((C, ROWS), F32)
    for k in range(8):
        picked = jnp.where(lane == k, sums[k * C : (k + 1) * C, :], picked)
    both = jnp.concatenate([picked, bias_sums[...], jnp.zeros((16, ROWS), F32)], axis=0)
    fold = ones_where((ROWS, 128), channel, lambda i: i, F32)
    folded = jnp.dot(both, fold, precision=HIGHEST, preferred_element_type=F32)
    for side in range(2):
        own[pl.ds(side * 5 + 4, KZT, stride=10), :] = folded


def last_own_kernel(
    own_in, modes, dmodes, depth_in, modes_in,
    part, spread_other, depth, grad_out,
    down_modes, wide, spread, grad, sems, out_sems,
):
    copies = start_copies(
        [(modes_in, down_modes), (depth_in.at[pl.ds(0, 3 * KZT)], depth)], sems
    )
    tiled = mm(wide_halves(by_mode(dmodes[...])), ones_where((2 * C, 128), channel, channel))
    expanded = mm(wide_halves(by_mode(modes[...])), ones_where((2 * C, C * C), channel, group))
    for j in range(8):
        grad[:, j * 128 : (j + 1) * 128] = expanded[:, j * 128 : (j + 1) * 128] * tiled
    leaving = pltpu.make_async_copy(grad, grad_out, out_sems.at[0])
    leaving.start()
    copies[0].wait()
    invert_own(own_in, 5, down_modes, part, spread_other, wide, spread)
    for copy in copies[1:]:
        copy.wait()
    leaving.wait()


def last_kernel(
    own_in, other_in, part, spread_other, dpre, depth, bypass,
    grad_out, grad_weight, grad_bias,
    grad, stack, mixing, sems,
):
    mixing[...] = block_mixing(bypass).astype(BF16)
    inverted = part[...] + mm(received_modes(other_in, 5).astype(BF16), spread_other[...])
    fill_stack(inverted, stack)
    total = own_in[pl.ds(4, KZT, stride=10), :] + other_in[pl.ds(4, KZT, stride=10), :]
    total = total * norm_scale
    grad_weight[...] = total[0:C, 0:C]
    grad_bias[...] = total[C : C + 1, 0:C]
    copies = [
        pltpu.make_async_copy(source, target, sems.at[i])
        for i, (source, target) in enumerate(block_pairs(grad, grad_out))
    ]
    for first in range(0, 8, 2):
        for i in (first, first + 1):
            spectral = mm_tn(stack[i // 4, :, block_rows(i % 4)], depth[...])
            grad[block_rows(i), :] = (spectral + mm(mixing[...], dpre[block_rows(i), :])).astype(BF16)
        copies[first].start()
        copies[first + 1].start()
    for copy in copies:
        copy.wait()


HELD = pl.BlockSpec(memory_space=pltpu.VMEM)
FAR = pl.BlockSpec(memory_space=pltpu.HBM)
SMEM = pl.BlockSpec(memory_space=pltpu.SMEM)
PARAMS = pltpu.CompilerParams(vmem_limit_bytes=24 * 1024 * 1024)


SHORT = pl.CostEstimate(flops=2 * 10**9, bytes_accessed=4 * 10**6, transcendentals=0)
LONG = pl.CostEstimate(flops=10**10, bytes_accessed=2 * 10**7, transcendentals=0)


def like(*shape, dtype=F32):
    return jax.ShapeDtypeStruct(shape, dtype)


def call(kernel, name, ins, outs, out_shape, scratch=(), cost=None):
    return pl.pallas_call(
        kernel,
        name=name,
        in_specs=ins,
        out_specs=outs,
        out_shape=out_shape,
        scratch_shapes=list(scratch),
        compiler_params=PARAMS,
        cost_estimate=cost,
    )


def swap_cores(value):
    return lax.ppermute(value, "gy", [(i, i ^ 1) for i in range(GY)])


def exchange(messages, lines):
    groups = [[(g * 2 + side) * 2 + core for g in range(GX) for side in range(2)] for core in range(2)]
    shaped = messages.reshape(128, 1, lines * 128)
    moved = lax.all_to_all(
        shaped, ("gx", "gy"), split_axis=0, concat_axis=0, tiled=True, axis_index_groups=groups
    )
    return moved.reshape(128 * lines, 128)


def far(value):
    return pltpu.with_memory_space_constraint(value, pltpu.HBM)


def local(layer_input, cotangent, spectral_weight, bypass_weight, channel_bias, hash_key):
    table = {name: jnp.asarray(value) for name, value in tables().items()}
    gather, scatter = table["gather"], table["scatter"]
    depth, down_cells, down_modes = (far(table[name]) for name in ("depth", "down_cells", "down_modes"))
    weight = spectral_weight.reshape(ROWS, C * C)
    field = far(layer_input.reshape(-1, LZT))
    field_far = pltpu.HBM((2048, LZT), BF16)
    held = lambda *shape, dtype=BF16: pltpu.VMEM(shape, dtype)
    sems = lambda count: pltpu.SemaphoreType.DMA((count,))
    field_held = held(2048, LZT)
    flat = held(2, 4, KZT, ROWS, dtype=F32)
    mixing = held(ROWS, ROWS)
    down = held(GY, 32, 32)
    wide = held(32, 1024, dtype=F32)
    half_rows = held(512, 1024)
    half_columns = held(1024, 512)
    part_like = like(128, 1024)
    cells_like = like(128, 1024, dtype=BF16)
    spread_like = like(512, 1024, dtype=BF16)
    field_like = like(2048, LZT, dtype=BF16)

    other, cells, wide_cells = call(
        forward_kernel,
        "forward",
        [FAR] * 3,
        [HELD] * 3,
        [like(512, 128), cells_like, like(32, 1024)],
        [field_held, held(KZT, LZT), down, half_columns, flat, sems(10)],
    )(field, depth, down_cells)
    arriving = swap_cores(other)
    own = call(forward_own_kernel, "forward_own", [HELD] * 2, HELD, like(512, 128), [half_columns], cost=SHORT)(
        cells, wide_cells
    )
    messages = exchange(own + arriving, 4)

    kept = call(
        prepare_kernel, "prepare", [SMEM, FAR], HELD, field_like, [field_held, sems(8)], cost=LONG
    )(hash_key, far(cotangent.reshape(-1, LZT)))
    messages, kept = lax.optimization_barrier((messages, kept))

    planes, modes = call(mix_kernel, "mix", [HELD] * 4, [HELD] * 2, [like(512, 128), like(KX, ROWS)])(
        messages, weight, gather, scatter
    )
    own_cells = exchange(planes, 4)
    other_cells = swap_cores(own_cells)
    part, spread_other, spread_cells, field_near, depth_near = call(
        middle_own_kernel,
        "middle_own",
        [HELD] + [FAR] * 4,
        [HELD] * 5,
        [
            part_like, spread_like, like(1024, 1024, dtype=BF16), like(8, KZT + ROWS + 16, LZT, dtype=BF16),
            like(3 * KZT + 16, LZT, dtype=BF16),
        ],
        [down, down, wide, wide, half_rows, sems(11)],
        SHORT,
    )(own_cells, field, depth, down_modes, down_cells)

    preact = held(ROWS, LZT, dtype=F32)
    other, cells, sums, bias_sums, dpre = call(
        middle_kernel,
        "middle",
        [HELD] * 9,
        [HELD] * 5,
        [like(640, 128), cells_like, like(ROWS, ROWS), like(16, ROWS), field_like],
        [held(2, 3 * KZT + 16, 1024), mixing, preact, preact, flat],
    )(
        other_cells, part, spread_other, spread_cells, field_near, kept, depth_near,
        channel_bias.reshape(1, C), bypass_weight,
    )
    arriving = swap_cores(other)
    own = call(middle_send_kernel, "middle_send", [HELD] * 4, HELD, like(640, 128), cost=SHORT)(
        cells, spread_cells, sums, bias_sums
    )
    messages = exchange(own + arriving, 5)

    planes, dmodes = call(back_kernel, "back", [HELD] * 4, [HELD] * 2, [like(640, 128), like(KX, ROWS)])(
        messages, weight, gather, scatter
    )
    own_cells = exchange(planes, 5)
    other_cells = swap_cores(own_cells)
    part, spread_other, depth_near, grad_spectral = call(
        last_own_kernel,
        "last_own",
        [HELD] * 3 + [FAR] * 2,
        [HELD] * 3 + [FAR],
        [part_like, spread_like, like(3 * KZT, LZT, dtype=BF16), pltpu.HBM((ROWS, 1024), F32)],
        [down, wide, half_rows, held(ROWS, 1024, dtype=F32), sems(10), sems(1)],
        SHORT,
    )(own_cells, modes, dmodes, depth, down_modes)

    grad_input, grad_weight, grad_bias = call(
        last_kernel,
        "last",
        [HELD] * 7,
        [FAR, HELD, HELD],
        [field_far, like(C, C), like(1, C)],
        [field_held, held(2, 3 * KZT, 1024), mixing, sems(8)],
    )(own_cells, other_cells, part, spread_other, dpre, depth_near, bypass_weight)
    return (
        grad_input.reshape(layer_input.shape),
        grad_spectral.reshape(spectral_weight.shape),
        grad_weight,
        grad_bias.reshape(C),
    )


def solution(mesh):
    return jax.shard_map(
        local,
        mesh=mesh,
        in_specs=(
            P("gx", "gy", None, None),
            P("gx", "gy", None, None),
            P("gy", "gx", None, None),
            P(),
            P(),
            P(),
        ),
        out_specs=(P("gx", "gy", None, None), P("gy", "gx", None, None), P(), P()),
        check_vma=False,
    )
```

```python
import math

import jax
import jax.numpy as jnp
import numpy as np
from jax import lax
from jax.experimental import pallas as pl
from jax.experimental.pallas import tpu as pltpu
from jax.sharding import PartitionSpec as P

LX = 128
LY = 128
LZ = 64
LT = 8
KX = 32
KY = 32
KZ = 16
KT = 4
C = 32
LZT = 512
KZT = 64
GX = 64
GY = 4
ROWS = 256
F32 = jnp.float32
BF16 = jnp.bfloat16
HIGHEST = lax.Precision.HIGHEST

keep_level = 6554
keep_scale = 1.0 / 0.9
gelu_cubic = 0.044715
mixer_one = -1640531535
mixer_two = -2048144789
mixer_three = -1028477387
norm_scale = 1.0 / math.sqrt(LX * LY * LZT)


def hartley_table(kept, length):
    wanted = np.arange(kept)
    frequency = np.where(wanted < kept // 2, wanted, wanted + (length - kept))
    residue = frequency[:, None] * np.arange(length)[None, :] % length
    radians = residue * (2.0 * math.pi / length)
    return ((np.cos(radians) + np.sin(radians)) / math.sqrt(length)).astype(np.float32)


def depth_table():
    joined = hartley_table(KZ, LZ)[:, None, :, None] * hartley_table(KT, LT)[None, :, None, :]
    return joined.reshape(KZT, LZT)


def split_table(table):
    high = table.astype(jnp.bfloat16)
    return high, (table - high.astype(np.float32)).astype(jnp.bfloat16)


def down_by_device():
    down = hartley_table(KY, LY)
    picked = []
    for q in range(GY):
        order = [
            ((side * 2 + (q % 2 + swap) % 2) * 8 + k)
            for swap in range(2)
            for side in range(2)
            for k in range(8)
        ]
        picked.append(down[order][:, q * 32 : (q + 1) * 32])
    return np.stack(picked)


def tables():
    down = down_by_device()
    low = lambda t: t.astype(jnp.bfloat16)
    depth = depth_table()
    depth_high, depth_rest = split_table(depth)
    across = hartley_table(KX, LX)
    gather = np.concatenate([np.repeat(across[:, x::2], 2, axis=1) for x in range(2)], axis=1)
    scatter = np.concatenate([across[:, x::2] for x in range(2)], axis=1)
    scatter_high, scatter_rest = split_table(scatter)
    scatter_stack = np.concatenate([scatter_high, scatter_high, scatter_rest], axis=0).T.copy()
    ones = np.concatenate([np.ones((3, LZT)), np.zeros((13, LZT))]).astype(jnp.bfloat16)
    return dict(
        down_cells=low(down.transpose(0, 2, 1)),
        down_modes=low(down),
        depth=np.concatenate([depth_high, depth_high, depth_rest, ones], axis=0),
        gather=np.concatenate(split_table(gather), axis=0),
        scatter=scatter_stack,
    )


def halves(value):
    high = value.astype(BF16)
    return high, (value - high.astype(F32)).astype(BF16)


def mm(a, b):
    return jnp.dot(a, b, preferred_element_type=F32)


def mm_nt(a, b):
    return lax.dot_general(a, b, (((1,), (1,)), ((), ())), preferred_element_type=F32)


def mm_tn(a, b):
    return lax.dot_general(a, b, (((0,), (0,)), ((), ())), preferred_element_type=F32)


def same(shape, rows, columns):
    row_ids = lax.broadcasted_iota(jnp.int32, shape, 0)
    column_ids = lax.broadcasted_iota(jnp.int32, shape, 1)
    return rows(row_ids) == columns(column_ids)


def ones_where(shape, rows, columns, dtype=BF16):
    return jnp.where(same(shape, rows, columns), 1.0, 0.0).astype(dtype)


def channel(index):
    return index & (C - 1)


def group(index):
    return index >> 5


def widen(table_ref):
    return mm(table_ref[lax.axis_index("gy")], ones_where((C, 32 * C), lambda i: i, group))


def fill_spread(wide_ref, columns, target_ref, first=0, count=32):
    mask = same((C, columns.stop - columns.start), lambda i: i, channel)
    for row in range(count):
        line = wide_ref[first + row : first + row + 1, columns]
        target_ref[row * C : (row + 1) * C, :] = jnp.where(mask, line, 0.0).astype(BF16)


OWN = slice(0, 512)
OTHER = slice(512, 1024)
ALL = slice(0, 1024)


def start_copies(pairs, sems):
    copies = [pltpu.make_async_copy(source, target, sems.at[i]) for i, (source, target) in enumerate(pairs)]
    for copy in copies:
        copy.start()
    return copies


def send_modes(modes, ref, lines):
    for side in range(2):
        for x in range(2):
            for half in range(2):
                at = (side * 2 + half) * 128
                ref[pl.ds(side * lines + x * 2 + half, KZT, stride=2 * lines), :] = modes[
                    x * KZT : (x + 1) * KZT, at : at + 128
                ]


def received_modes(ref, lines):
    rows = []
    for x in range(2):
        parts = [
            ref[pl.ds(side * lines + x * 2 + half, KZT, stride=2 * lines), :]
            for side in range(2)
            for half in range(2)
        ]
        rows.append(jnp.concatenate(parts, axis=1))
    return jnp.concatenate(rows, axis=0)


def block_mixing(weight_ref):
    weight = weight_ref[...].astype(F32)
    wide = jnp.concatenate([weight] * 8, axis=1)
    full = jnp.concatenate([wide] * 8, axis=0)
    return jnp.where(same((ROWS, ROWS), group, group), full, 0.0)


def fill_stack(cells, stack_ref):
    high, rest = halves(cells)
    for x in range(2):
        part = slice(x * KZT, (x + 1) * KZT)
        stack_ref[x, 0:KZT, :] = high[part]
        stack_ref[x, KZT : 2 * KZT, :] = rest[part]
        stack_ref[x, 2 * KZT : 3 * KZT, :] = high[part]


def block_rows(i):
    return slice(i * ROWS, (i + 1) * ROWS)


def block_pairs(source, target):
    return [(source.at[pl.ds(i * ROWS, ROWS)], target.at[pl.ds(i * ROWS, ROWS)]) for i in range(8)]


def forward_kernel(field_in, depth_in, down_in, other, cells, wide, field, depth, down, spread, flat, sems):
    copies = start_copies(
        [(down_in, down), (depth_in.at[pl.ds(0, KZT)], depth)] + block_pairs(field_in, field), sems
    )
    copies[0].wait()
    wide[...] = widen(down)
    fill_spread(wide, OTHER, spread)
    copies[1].wait()
    for first in (0, 4):
        for i in range(first, first + 4):
            copies[2 + i].wait()
        for i in range(first, first + 4):
            flat[i // 4, i % 4] = mm_nt(depth[...], field[block_rows(i), :])
    cells[...] = joined(flat).astype(BF16)
    send_modes(mm(cells[...], spread[...]), other, 4)


def forward_own_kernel(cells, wide, own, spread):
    fill_spread(wide, OWN, spread)
    send_modes(mm(cells[...], spread[...]), own, 4)


def joined(flat):
    return jnp.concatenate(
        [jnp.concatenate([flat[x, block] for block in range(4)], axis=1) for x in range(2)], axis=0
    )


def scramble(hashed):
    hashed = jnp.bitwise_xor(hashed, lax.shift_right_logical(hashed, jnp.int32(16)))
    hashed = hashed * jnp.int32(mixer_two)
    hashed = jnp.bitwise_xor(hashed, lax.shift_right_logical(hashed, jnp.int32(13)))
    hashed = hashed * jnp.int32(mixer_three)
    return jnp.bitwise_xor(hashed, lax.shift_right_logical(hashed, jnp.int32(16)))


def prepare_kernel(
    key, cotangent_in, down_in, bypass, kept, mixing, mixing_turned, wide, cotangent, down, in_sems, down_sem
):
    narrow = start_copies([(down_in, down)], down_sem)[0]
    arriving = start_copies(block_pairs(cotangent_in, cotangent), in_sems)
    blocks = block_mixing(bypass)
    mixing[...] = blocks.astype(BF16)
    mixing_turned[...] = jnp.transpose(blocks).astype(BF16)
    narrow.wait()
    wide[...] = widen(down)
    origin = (lax.axis_index("gx") * 2 * LY + lax.axis_index("gy") * 32) * (C * LZT)
    shape = (16, LZT)
    inside = (
        lax.broadcasted_iota(jnp.int32, shape, 0) * LZT + lax.broadcasted_iota(jnp.int32, shape, 1)
    ) * jnp.int32(mixer_one)
    for i in range(8):
        first = origin + ((i // 4) * LY + (i % 4) * 8) * (C * LZT)
        arriving[i].wait()

        def body(chunk, carry):
            for part in range(4):
                at = chunk * 64 + part * 16
                start = (first + at * LZT) * jnp.int32(mixer_one) + key[0]
                hashed = scramble(inside + start)
                hashed = scramble(jnp.bitwise_xor(hashed, key[1]))
                keep = jnp.bitwise_and(hashed, jnp.int32(65535)) >= keep_level
                rows = pl.ds(pl.multiple_of(i * ROWS + at, 16), 16)
                kept[rows, :] = jnp.where(keep, cotangent[rows, :].astype(F32), 0.0).astype(BF16)
            return carry

        lax.fori_loop(0, 4, body, 0)


def gathered_modes(messages, gather, lines):
    slabs = [
        jnp.concatenate([messages[pl.ds(x * 2 + half, 128, stride=lines), :] for half in range(2)], axis=1)
        for x in range(2)
    ]
    high, rest = halves(jnp.concatenate(slabs, axis=0))
    both = mm(gather[...], high)
    return both[0:KX] + both[KX : 2 * KX] + mm(gather[0:KX, :], rest)


def by_mode(modes):
    return jnp.concatenate([modes[:, k * C : (k + 1) * C] for k in range(8)], axis=0)


def wide_halves(value):
    return jnp.concatenate(halves(value), axis=1)


def scatter_planes(repeated, scatter, out, lines):
    lane = lax.broadcasted_iota(jnp.int32, (KX, ROWS), 1) >> 5
    modes = jnp.zeros((KX, ROWS), F32)
    for k in range(8):
        modes = jnp.where(lane == k, repeated[k * KX : (k + 1) * KX, :], modes)
    high, rest = halves(modes)
    planes = mm(scatter[...], jnp.concatenate([high, rest, high], axis=0))
    for x in range(2):
        for half in range(2):
            piece = planes[x * GX : (x + 1) * GX, half * 128 : (half + 1) * 128]
            for side in range(2):
                out[pl.ds(side * lines + x * 2 + half, GX, stride=2 * lines), :] = piece


def mix_kernel(messages, weight, gather, scatter, out, modes_out):
    modes = gathered_modes(messages, gather, 4)
    modes_out[...] = modes
    spread = mm(wide_halves(by_mode(modes)), ones_where((2 * C, C * C), channel, group))
    total = jnp.zeros((ROWS, 128), F32)
    for j in range(8):
        part = slice(j * 128, (j + 1) * 128)
        total = total + spread[:, part] * weight[:, part].astype(F32)
    repeated = mm(wide_halves(total), ones_where((256, 256), channel, channel))
    scatter_planes(repeated, scatter, out, 4)


def back_kernel(messages, weight, gather, scatter, out, dmodes_out):
    dmodes = gathered_modes(messages, gather, 5)
    dmodes_out[...] = dmodes
    tiled = mm(wide_halves(by_mode(dmodes)), ones_where((2 * C, 128), channel, channel))
    repeated = jnp.zeros((ROWS, ROWS), F32)
    for j in range(8):
        product = (weight[:, j * 128 : (j + 1) * 128].astype(F32) * tiled).astype(BF16)
        repeated = repeated + mm(product, ones_where((128, 256), lambda i: group(i) + 4 * j, channel))
    scatter_planes(repeated, scatter, out, 5)
    total = jnp.sum(messages[pl.ds(4, 128, stride=5), :], axis=0, keepdims=True)
    out[pl.ds(4, 128, stride=5), :] = jnp.broadcast_to(total, (128, 128))


def scaled_slope(preact):
    factor = math.sqrt(2.0 / math.pi)
    square = preact * preact
    tanh_value = jnp.tanh(preact * (factor + (factor * gelu_cubic) * square))
    half = 0.5 * keep_scale
    rest = preact * (half * factor + (half * 3.0 * factor * gelu_cubic) * square)
    return (1.0 + tanh_value) * (half + rest * (1.0 - tanh_value))


def invert_own(own_in, lines, wide, part, spread_other, spread):
    fill_spread(wide, ALL, spread, 0, 16)
    part[...] = mm(received_modes(own_in, lines).astype(BF16), spread[...])
    fill_spread(wide, ALL, spread_other, 16, 16)


def middle_own_kernel(
    own_in, wide_modes, wide_cells, field_in, depth_in,
    part, spread_other, spread_cells, field, depth,
    spread, sems,
):
    copies = start_copies(
        [(depth_in, depth)]
        + [(field_in.at[pl.ds(i * ROWS, ROWS)], field.at[i, pl.ds(KZT, ROWS)]) for i in range(8)],
        sems,
    )
    invert_own(own_in, 4, wide_modes, part, spread_other, spread)
    fill_spread(wide_cells, OTHER, spread_cells)
    copies[0].wait()
    for i in range(8):
        field[i, 0:KZT, :] = depth[0:KZT, :]
        field[i, KZT + ROWS :, :] = jnp.ones((16, LZT), BF16)
    for copy in copies[1:]:
        copy.wait()


def middle_kernel(
    other_in, part, spread_other, spread_cells, field, kept, depth, bias, mixing,
    other, cells, sums, bias_sums, dpre,
    stack, preact_even, preact_odd, flat,
):
    sums[...] = jnp.zeros_like(sums)
    bias_sums[...] = jnp.zeros_like(bias_sums)
    inverted = part[...] + mm(received_modes(other_in, 4).astype(BF16), spread_other[...])
    fill_stack(inverted, stack)
    first = bias[...]
    bias_high = first.astype(BF16)
    bias_rest, bias_last = halves(first - bias_high.astype(F32))
    lines = jnp.concatenate([bias_high, bias_rest, bias_last], axis=0).astype(F32)
    lines = jnp.concatenate([lines, jnp.zeros((13, C), F32)], axis=0).astype(BF16)
    wide_bias = mm(lines, ones_where((C, 32 * C), lambda i: i, channel)).astype(BF16)
    for x in range(2):
        stack[x, 3 * KZT : 3 * KZT + 16, :] = wide_bias
    preacts = (preact_even, preact_odd)

    def linear(i):
        spectral = mm_tn(stack[i // 4, :, block_rows(i % 4)], depth[...])
        preacts[i % 2][...] = spectral + mm(mixing[...], field[i, KZT : KZT + ROWS, :])

    def activate(i):
        for chunk in range(ROWS // 16):
            rows = slice(i * ROWS + chunk * 16, i * ROWS + chunk * 16 + 16)
            slope = scaled_slope(preacts[i % 2][chunk * 16 : chunk * 16 + 16, :])
            dpre[rows, :] = (kept[rows, :].astype(F32) * slope).astype(BF16)

    def reduce(i):
        found = mm_nt(field[i], dpre[block_rows(i), :])
        flat[i // 4, i % 4] = found[0:KZT]
        sums[...] += found[KZT : KZT + ROWS]
        bias_sums[...] += found[KZT + ROWS :]

    linear(0)
    for i in range(9):
        if i < 7:
            linear(i + 1)
        if i > 0:
            reduce(i - 1)
        if i < 8:
            activate(i)

    cells[...] = joined(flat).astype(BF16)
    send_modes(mm(cells[...], spread_cells[...]), other, 5)
    for side in range(2):
        other[pl.ds(side * 5 + 4, KZT, stride=10), :] = jnp.zeros((KZT, 128), F32)


def middle_send_kernel(cells, wide_cells, sums, bias_sums, own, spread):
    fill_spread(wide_cells, OWN, spread)
    send_modes(mm(cells[...], spread[...]), own, 5)
    lane = lax.broadcasted_iota(jnp.int32, (C, ROWS), 1) >> 5
    picked = jnp.zeros((C, ROWS), F32)
    for k in range(8):
        picked = jnp.where(lane == k, sums[k * C : (k + 1) * C, :], picked)
    both = jnp.concatenate([picked, bias_sums[...], jnp.zeros((16, ROWS), F32)], axis=0)
    fold = ones_where((ROWS, 128), channel, lambda i: i, F32)
    folded = jnp.dot(both, fold, precision=HIGHEST, preferred_element_type=F32)
    for side in range(2):
        own[pl.ds(side * 5 + 4, KZT, stride=10), :] = folded


def last_own_kernel(
    own_in, modes, dmodes, wide_modes, depth_in,
    part, spread_other, depth, grad_out,
    spread, grad, sems,
):
    arriving = pltpu.make_async_copy(depth_in.at[pl.ds(0, 3 * KZT)], depth, sems.at[0])
    arriving.start()
    tiled = mm(wide_halves(by_mode(dmodes[...])), ones_where((2 * C, 128), channel, channel))
    expanded = mm(wide_halves(by_mode(modes[...])), ones_where((2 * C, C * C), channel, group))
    for j in range(8):
        grad[:, j * 128 : (j + 1) * 128] = expanded[:, j * 128 : (j + 1) * 128] * tiled
    leaving = pltpu.make_async_copy(grad, grad_out, sems.at[1])
    leaving.start()
    invert_own(own_in, 5, wide_modes, part, spread_other, spread)
    arriving.wait()
    leaving.wait()


def last_kernel(
    own_in, other_in, part, spread_other, dpre, depth, mixing,
    grad_out, grad_weight, grad_bias,
    grad, stack, sems,
):
    inverted = part[...] + mm(received_modes(other_in, 5).astype(BF16), spread_other[...])
    fill_stack(inverted, stack)
    total = own_in[pl.ds(4, KZT, stride=10), :] + other_in[pl.ds(4, KZT, stride=10), :]
    total = total * norm_scale
    grad_weight[...] = total[0:C, 0:C]
    grad_bias[...] = total[C : C + 1, 0:C]
    copies = [
        pltpu.make_async_copy(source, target, sems.at[i])
        for i, (source, target) in enumerate(block_pairs(grad, grad_out))
    ]
    for i in range(8):
        spectral = mm_tn(stack[i // 4, :, block_rows(i % 4)], depth[...])
        grad[block_rows(i), :] = (spectral + mm(mixing[...], dpre[block_rows(i), :])).astype(BF16)
        copies[i].start()
    for copy in copies:
        copy.wait()


HELD = pl.BlockSpec(memory_space=pltpu.VMEM)
FAR = pl.BlockSpec(memory_space=pltpu.HBM)
SMEM = pl.BlockSpec(memory_space=pltpu.SMEM)
PARAMS = pltpu.CompilerParams(vmem_limit_bytes=24 * 1024 * 1024)


SHORT = pl.CostEstimate(flops=2 * 10**9, bytes_accessed=4 * 10**6, transcendentals=0)
LONG = pl.CostEstimate(flops=10**10, bytes_accessed=2 * 10**7, transcendentals=0)


def like(*shape, dtype=F32):
    return jax.ShapeDtypeStruct(shape, dtype)


def call(kernel, name, ins, outs, out_shape, scratch=(), cost=None):
    return pl.pallas_call(
        kernel,
        name=name,
        in_specs=ins,
        out_specs=outs,
        out_shape=out_shape,
        scratch_shapes=list(scratch),
        compiler_params=PARAMS,
        cost_estimate=cost,
    )


def swap_cores(value):
    return lax.ppermute(value, "gy", [(i, i ^ 1) for i in range(GY)])


def exchange(messages, lines):
    groups = [[(g * 2 + side) * 2 + core for g in range(GX) for side in range(2)] for core in range(2)]
    shaped = messages.reshape(128, 1, lines * 128)
    moved = lax.all_to_all(
        shaped, ("gx", "gy"), split_axis=0, concat_axis=0, tiled=True, axis_index_groups=groups
    )
    return moved.reshape(128 * lines, 128)


def far(value):
    return pltpu.with_memory_space_constraint(value, pltpu.HBM)


def local(layer_input, cotangent, spectral_weight, bypass_weight, channel_bias, hash_key):
    table = {name: jnp.asarray(value) for name, value in tables().items()}
    gather, scatter = table["gather"], table["scatter"]
    depth, down_cells, down_modes = (far(table[name]) for name in ("depth", "down_cells", "down_modes"))
    weight = spectral_weight.reshape(ROWS, C * C)
    field = far(layer_input.reshape(-1, LZT))
    field_far = pltpu.HBM((2048, LZT), BF16)
    held = lambda *shape, dtype=BF16: pltpu.VMEM(shape, dtype)
    sems = lambda count: pltpu.SemaphoreType.DMA((count,))
    field_held = held(2048, LZT)
    flat = held(2, 4, KZT, ROWS, dtype=F32)
    down = held(GY, 32, 32)
    half_rows = held(512, 1024)
    half_columns = held(1024, 512)
    part_like = like(128, 1024)
    cells_like = like(128, 1024, dtype=BF16)
    spread_like = like(512, 1024, dtype=BF16)
    field_like = like(2048, LZT, dtype=BF16)

    other, cells, wide_cells = call(
        forward_kernel,
        "forward",
        [FAR] * 3,
        [HELD] * 3,
        [like(512, 128), cells_like, like(32, 1024)],
        [field_held, held(KZT, LZT), down, half_columns, flat, sems(10)],
    )(field, depth, down_cells)
    arriving = swap_cores(other)
    own = call(forward_own_kernel, "forward_own", [HELD] * 2, HELD, like(512, 128), [half_columns], cost=SHORT)(
        cells, wide_cells
    )
    messages = exchange(own + arriving, 4)

    mixing_like = like(ROWS, ROWS, dtype=BF16)
    prepared = call(
        prepare_kernel,
        "prepare",
        [SMEM, FAR, FAR, HELD],
        [HELD] * 4,
        [field_like, mixing_like, mixing_like, like(32, 1024)],
        [field_held, down, sems(8), sems(1)],
        LONG,
    )(hash_key, far(cotangent.reshape(-1, LZT)), down_modes, bypass_weight)
    messages, (kept, mixing, mixing_turned, wide_modes) = lax.optimization_barrier((messages, prepared))

    planes, modes = call(mix_kernel, "mix", [HELD] * 4, [HELD] * 2, [like(512, 128), like(KX, ROWS)])(
        messages, weight, gather, scatter
    )
    own_cells = exchange(planes, 4)
    other_cells = swap_cores(own_cells)
    part, spread_other, spread_cells, field_near, depth_near = call(
        middle_own_kernel,
        "middle_own",
        [HELD] * 3 + [FAR] * 2,
        [HELD] * 5,
        [
            part_like, spread_like, like(1024, 512, dtype=BF16), like(8, KZT + ROWS + 16, LZT, dtype=BF16),
            like(3 * KZT + 16, LZT, dtype=BF16),
        ],
        [half_rows, sems(9)],
        SHORT,
    )(own_cells, wide_modes, wide_cells, field, depth)

    preact = held(ROWS, LZT, dtype=F32)
    other, cells, sums, bias_sums, dpre = call(
        middle_kernel,
        "middle",
        [HELD] * 9,
        [HELD] * 5,
        [like(640, 128), cells_like, like(ROWS, ROWS), like(16, ROWS), field_like],
        [held(2, 3 * KZT + 16, 1024), preact, preact, flat],
    )(
        other_cells, part, spread_other, spread_cells, field_near, kept, depth_near,
        channel_bias.reshape(1, C), mixing_turned,
    )
    arriving = swap_cores(other)
    own = call(middle_send_kernel, "middle_send", [HELD] * 4, HELD, like(640, 128), [half_columns], SHORT)(
        cells, wide_cells, sums, bias_sums
    )
    messages = exchange(own + arriving, 5)

    planes, dmodes = call(back_kernel, "back", [HELD] * 4, [HELD] * 2, [like(640, 128), like(KX, ROWS)])(
        messages, weight, gather, scatter
    )
    own_cells = exchange(planes, 5)
    other_cells = swap_cores(own_cells)
    part, spread_other, depth_near, grad_spectral = call(
        last_own_kernel,
        "last_own",
        [HELD] * 4 + [FAR],
        [HELD] * 3 + [FAR],
        [part_like, spread_like, like(3 * KZT, LZT, dtype=BF16), pltpu.HBM((ROWS, 1024), F32)],
        [half_rows, held(ROWS, 1024, dtype=F32), sems(2)],
        SHORT,
    )(own_cells, modes, dmodes, wide_modes, depth)

    grad_input, grad_weight, grad_bias = call(
        last_kernel,
        "last",
        [HELD] * 7,
        [FAR, HELD, HELD],
        [field_far, like(C, C), like(1, C)],
        [field_held, held(2, 3 * KZT, 1024), sems(8)],
    )(own_cells, other_cells, part, spread_other, dpre, depth_near, mixing)
    return (
        grad_input.reshape(layer_input.shape),
        grad_spectral.reshape(spectral_weight.shape),
        grad_weight,
        grad_bias.reshape(C),
    )


def solution(mesh):
    return jax.shard_map(
        local,
        mesh=mesh,
        in_specs=(
            P("gx", "gy", None, None),
            P("gx", "gy", None, None),
            P("gy", "gx", None, None),
            P(),
            P(),
            P(),
        ),
        out_specs=(P("gx", "gy", None, None), P("gy", "gx", None, None), P(), P()),
        check_vma=False,
    )
```

```python
import math

import jax
import jax.numpy as jnp
import numpy as np
from jax import lax
from jax.experimental import pallas as pl
from jax.experimental.pallas import tpu as pltpu
from jax.sharding import PartitionSpec as P

LX = 128
LY = 128
LZ = 64
LT = 8
KX = 32
KY = 32
KZ = 16
KT = 4
C = 32
LZT = 512
KZT = 64
GX = 64
GY = 4
ROWS = 256
F32 = jnp.float32
BF16 = jnp.bfloat16
HIGHEST = lax.Precision.HIGHEST

keep_level = 6554
keep_scale = 1.0 / 0.9
gelu_cubic = 0.044715
mixer_one = -1640531535
mixer_two = -2048144789
mixer_three = -1028477387
norm_scale = 1.0 / math.sqrt(LX * LY * LZT)


def hartley_table(kept, length):
    wanted = np.arange(kept)
    frequency = np.where(wanted < kept // 2, wanted, wanted + (length - kept))
    residue = frequency[:, None] * np.arange(length)[None, :] % length
    radians = residue * (2.0 * math.pi / length)
    return ((np.cos(radians) + np.sin(radians)) / math.sqrt(length)).astype(np.float32)


def depth_table():
    joined = hartley_table(KZ, LZ)[:, None, :, None] * hartley_table(KT, LT)[None, :, None, :]
    return joined.reshape(KZT, LZT)


def split_table(table):
    high = table.astype(jnp.bfloat16)
    return high, (table - high.astype(np.float32)).astype(jnp.bfloat16)


def down_by_device():
    down = hartley_table(KY, LY)
    picked = []
    for q in range(GY):
        order = [
            ((side * 2 + (q % 2 + swap) % 2) * 8 + k)
            for swap in range(2)
            for side in range(2)
            for k in range(8)
        ]
        picked.append(down[order][:, q * 32 : (q + 1) * 32])
    return np.stack(picked)


def tables():
    down = down_by_device()
    low = lambda t: t.astype(jnp.bfloat16)
    depth = depth_table()
    depth_high, depth_rest = split_table(depth)
    across = hartley_table(KX, LX)
    gather = np.concatenate([np.repeat(across[:, x::2], 2, axis=1) for x in range(2)], axis=1)
    scatter = np.concatenate([across[:, x::2] for x in range(2)], axis=1)
    scatter_high, scatter_rest = split_table(scatter)
    scatter_stack = np.concatenate([scatter_high, scatter_high, scatter_rest], axis=0).T.copy()
    ones = np.concatenate([np.ones((3, LZT)), np.zeros((13, LZT))]).astype(jnp.bfloat16)
    return dict(
        down_cells=low(down.transpose(0, 2, 1)),
        down_modes=low(down),
        depth=np.concatenate([depth_high, depth_high, depth_rest, ones], axis=0),
        gather=np.concatenate(split_table(gather), axis=0),
        scatter=scatter_stack,
    )


def halves(value):
    high = value.astype(BF16)
    return high, (value - high.astype(F32)).astype(BF16)


def mm(a, b):
    return jnp.dot(a, b, preferred_element_type=F32)


def mm_nt(a, b):
    return lax.dot_general(a, b, (((1,), (1,)), ((), ())), preferred_element_type=F32)


def mm_tn(a, b):
    return lax.dot_general(a, b, (((0,), (0,)), ((), ())), preferred_element_type=F32)


def same(shape, rows, columns):
    row_ids = lax.broadcasted_iota(jnp.int32, shape, 0)
    column_ids = lax.broadcasted_iota(jnp.int32, shape, 1)
    return rows(row_ids) == columns(column_ids)


def ones_where(shape, rows, columns, dtype=BF16):
    return jnp.where(same(shape, rows, columns), 1.0, 0.0).astype(dtype)


def channel(index):
    return index & (C - 1)


def group(index):
    return index >> 5


def widen(table_ref):
    return mm(table_ref[lax.axis_index("gy")], ones_where((C, 32 * C), lambda i: i, group))


def fill_spread(wide_ref, columns, target_ref, first=0, count=32):
    mask = same((C, columns.stop - columns.start), lambda i: i, channel)
    for row in range(count):
        line = wide_ref[first + row : first + row + 1, columns]
        target_ref[row * C : (row + 1) * C, :] = jnp.where(mask, line, 0.0).astype(BF16)


OWN = slice(0, 512)
OTHER = slice(512, 1024)
ALL = slice(0, 1024)


def start_copies(pairs, sems):
    copies = [pltpu.make_async_copy(source, target, sems.at[i]) for i, (source, target) in enumerate(pairs)]
    for copy in copies:
        copy.start()
    return copies


def send_modes(modes, ref, lines):
    for side in range(2):
        for x in range(2):
            for half in range(2):
                at = (side * 2 + half) * 128
                ref[pl.ds(side * lines + x * 2 + half, KZT, stride=2 * lines), :] = modes[
                    x * KZT : (x + 1) * KZT, at : at + 128
                ]


def received_modes(ref, lines):
    rows = []
    for x in range(2):
        parts = [
            ref[pl.ds(side * lines + x * 2 + half, KZT, stride=2 * lines), :]
            for side in range(2)
            for half in range(2)
        ]
        rows.append(jnp.concatenate(parts, axis=1))
    return jnp.concatenate(rows, axis=0)


def block_mixing(weight_ref):
    weight = weight_ref[...].astype(F32)
    wide = jnp.concatenate([weight] * 8, axis=1)
    full = jnp.concatenate([wide] * 8, axis=0)
    return jnp.where(same((ROWS, ROWS), group, group), full, 0.0)


def fill_stack(cells, stack_ref):
    high, rest = halves(cells)
    for x in range(2):
        part = slice(x * KZT, (x + 1) * KZT)
        stack_ref[x, 0:KZT, :] = high[part]
        stack_ref[x, KZT : 2 * KZT, :] = rest[part]
        stack_ref[x, 2 * KZT : 3 * KZT, :] = high[part]


def block_rows(i):
    return slice(i * ROWS, (i + 1) * ROWS)


def block_pairs(source, target):
    return [(source.at[pl.ds(i * ROWS, ROWS)], target.at[pl.ds(i * ROWS, ROWS)]) for i in range(8)]


def forward_kernel(field_in, depth_in, down_in, other, cells, wide, field, depth, down, spread, flat, sems):
    copies = start_copies(
        [(down_in, down), (depth_in.at[pl.ds(0, KZT)], depth)] + block_pairs(field_in, field), sems
    )
    copies[0].wait()
    wide[...] = widen(down)
    fill_spread(wide, OTHER, spread)
    copies[1].wait()
    for first in (0, 4):
        for i in range(first, first + 4):
            copies[2 + i].wait()
        for i in range(first, first + 4):
            flat[i // 4, i % 4] = mm_nt(depth[...], field[block_rows(i), :])
    cells[...] = joined(flat).astype(BF16)
    send_modes(mm(cells[...], spread[...]), other, 4)


def forward_own_kernel(cells, wide, own, spread):
    fill_spread(wide, OWN, spread)
    send_modes(mm(cells[...], spread[...]), own, 4)


def joined(flat):
    return jnp.concatenate(
        [jnp.concatenate([flat[x, block] for block in range(4)], axis=1) for x in range(2)], axis=0
    )


def scramble(hashed):
    hashed = jnp.bitwise_xor(hashed, lax.shift_right_logical(hashed, jnp.int32(16)))
    hashed = hashed * jnp.int32(mixer_two)
    hashed = jnp.bitwise_xor(hashed, lax.shift_right_logical(hashed, jnp.int32(13)))
    hashed = hashed * jnp.int32(mixer_three)
    return jnp.bitwise_xor(hashed, lax.shift_right_logical(hashed, jnp.int32(16)))


def prepare_kernel(
    key, cotangent_in, down_in, bypass, bias,
    kept, mixing, mixing_turned, wide, wide_bias,
    cotangent, down, in_sems, down_sem,
):
    narrow = start_copies([(down_in, down)], down_sem)[0]
    arriving = start_copies(block_pairs(cotangent_in, cotangent), in_sems)
    first = bias[...]
    bias_high = first.astype(BF16)
    bias_rest, bias_last = halves(first - bias_high.astype(F32))
    lines = jnp.concatenate([bias_high, bias_rest, bias_last], axis=0).astype(F32)
    lines = jnp.concatenate([lines, jnp.zeros((13, C), F32)], axis=0).astype(BF16)
    wide_bias[...] = mm(lines, ones_where((C, 32 * C), lambda i: i, channel)).astype(BF16)
    blocks = block_mixing(bypass)
    mixing[...] = blocks.astype(BF16)
    mixing_turned[...] = jnp.transpose(blocks).astype(BF16)
    narrow.wait()
    wide[...] = widen(down)
    origin = (lax.axis_index("gx") * 2 * LY + lax.axis_index("gy") * 32) * (C * LZT)
    shape = (16, LZT)
    inside = (
        lax.broadcasted_iota(jnp.int32, shape, 0) * LZT + lax.broadcasted_iota(jnp.int32, shape, 1)
    ) * jnp.int32(mixer_one)
    for i in range(8):
        first = origin + ((i // 4) * LY + (i % 4) * 8) * (C * LZT)
        arriving[i].wait()

        def body(chunk, carry):
            for part in range(4):
                at = chunk * 64 + part * 16
                start = (first + at * LZT) * jnp.int32(mixer_one) + key[0]
                hashed = scramble(inside + start)
                hashed = scramble(jnp.bitwise_xor(hashed, key[1]))
                keep = jnp.bitwise_and(hashed, jnp.int32(65535)) >= keep_level
                rows = pl.ds(pl.multiple_of(i * ROWS + at, 16), 16)
                kept[rows, :] = jnp.where(keep, cotangent[rows, :].astype(F32), 0.0).astype(BF16)
            return carry

        lax.fori_loop(0, 4, body, 0)


def gathered_modes(messages, gather, lines):
    slabs = [
        jnp.concatenate([messages[pl.ds(x * 2 + half, 128, stride=lines), :] for half in range(2)], axis=1)
        for x in range(2)
    ]
    high, rest = halves(jnp.concatenate(slabs, axis=0))
    both = mm(gather[...], high)
    return both[0:KX] + both[KX : 2 * KX] + mm(gather[0:KX, :], rest)


def by_mode(modes):
    return jnp.concatenate([modes[:, k * C : (k + 1) * C] for k in range(8)], axis=0)


def wide_halves(value):
    return jnp.concatenate(halves(value), axis=1)


def scatter_planes(repeated, scatter, out, lines):
    lane = lax.broadcasted_iota(jnp.int32, (KX, ROWS), 1) >> 5
    modes = jnp.zeros((KX, ROWS), F32)
    for k in range(8):
        modes = jnp.where(lane == k, repeated[k * KX : (k + 1) * KX, :], modes)
    high, rest = halves(modes)
    planes = mm(scatter[...], jnp.concatenate([high, rest, high], axis=0))
    for x in range(2):
        for half in range(2):
            piece = planes[x * GX : (x + 1) * GX, half * 128 : (half + 1) * 128]
            for side in range(2):
                out[pl.ds(side * lines + x * 2 + half, GX, stride=2 * lines), :] = piece


def mix_kernel(messages, weight, gather, scatter, out, modes_out):
    modes = gathered_modes(messages, gather, 4)
    modes_out[...] = modes
    spread = mm(wide_halves(by_mode(modes)), ones_where((2 * C, C * C), channel, group))
    total = jnp.zeros((ROWS, 128), F32)
    for j in range(8):
        part = slice(j * 128, (j + 1) * 128)
        total = total + spread[:, part] * weight[:, part].astype(F32)
    repeated = mm(wide_halves(total), ones_where((256, 256), channel, channel))
    scatter_planes(repeated, scatter, out, 4)


def back_kernel(messages, weight, gather, scatter, out, dmodes_out):
    dmodes = gathered_modes(messages, gather, 5)
    dmodes_out[...] = dmodes
    tiled = mm(wide_halves(by_mode(dmodes)), ones_where((2 * C, 128), channel, channel))
    repeated = jnp.zeros((ROWS, ROWS), F32)
    for j in range(8):
        product = (weight[:, j * 128 : (j + 1) * 128].astype(F32) * tiled).astype(BF16)
        repeated = repeated + mm(product, ones_where((128, 256), lambda i: group(i) + 4 * j, channel))
    scatter_planes(repeated, scatter, out, 5)
    total = jnp.sum(messages[pl.ds(4, 128, stride=5), :], axis=0, keepdims=True)
    out[pl.ds(4, 128, stride=5), :] = jnp.broadcast_to(total, (128, 128))


def scaled_slope(preact):
    factor = math.sqrt(2.0 / math.pi)
    square = preact * preact
    tanh_value = jnp.tanh(preact * (factor + (factor * gelu_cubic) * square))
    half = 0.5 * keep_scale
    rest = preact * (half * factor + (half * 3.0 * factor * gelu_cubic) * square)
    return (1.0 + tanh_value) * (half + rest * (1.0 - tanh_value))


def invert_own(own_in, lines, wide, part, spread_other, spread):
    fill_spread(wide, ALL, spread, 0, 16)
    part[...] = mm(received_modes(own_in, lines).astype(BF16), spread[...])
    fill_spread(wide, ALL, spread_other, 16, 16)


def middle_own_kernel(
    own_in, wide_modes, wide_cells, field_in, depth_in,
    part, spread_other, spread_cells, field, depth,
    spread, sems,
):
    copies = start_copies(
        [(depth_in, depth)]
        + [(field_in.at[pl.ds(i * ROWS, ROWS)], field.at[i, pl.ds(KZT, ROWS)]) for i in range(8)],
        sems,
    )
    invert_own(own_in, 4, wide_modes, part, spread_other, spread)
    fill_spread(wide_cells, OTHER, spread_cells)
    copies[0].wait()
    for i in range(8):
        field[i, 0:KZT, :] = depth[0:KZT, :]
        field[i, KZT + ROWS :, :] = jnp.ones((16, LZT), BF16)
    for copy in copies[1:]:
        copy.wait()


def middle_kernel(
    other_in, part, spread_other, spread_cells, field, kept, depth, wide_bias, mixing,
    other, cells, sums, bias_sums, dpre,
    stack, preact_even, preact_odd, flat,
):
    sums[...] = jnp.zeros_like(sums)
    bias_sums[...] = jnp.zeros_like(bias_sums)
    inverted = part[...] + mm(received_modes(other_in, 4).astype(BF16), spread_other[...])
    fill_stack(inverted, stack)
    for x in range(2):
        stack[x, 3 * KZT : 3 * KZT + 16, :] = wide_bias[...]
    preacts = (preact_even, preact_odd)

    def linear(i):
        spectral = mm_tn(stack[i // 4, :, block_rows(i % 4)], depth[...])
        preacts[i % 2][...] = spectral + mm(mixing[...], field[i, KZT : KZT + ROWS, :])

    def activate(i):
        for chunk in range(ROWS // 32):
            rows = slice(i * ROWS + chunk * 32, i * ROWS + chunk * 32 + 32)
            slope = scaled_slope(preacts[i % 2][chunk * 32 : chunk * 32 + 32, :])
            dpre[rows, :] = (kept[rows, :].astype(F32) * slope).astype(BF16)

    def reduce(i):
        found = mm_nt(field[i], dpre[block_rows(i), :])
        flat[i // 4, i % 4] = found[0:KZT]
        sums[...] += found[KZT : KZT + ROWS]
        bias_sums[...] += found[KZT + ROWS :]

    linear(0)
    for i in range(9):
        if i < 7:
            linear(i + 1)
        if i > 0:
            reduce(i - 1)
        if i < 8:
            activate(i)

    cells[...] = joined(flat).astype(BF16)
    send_modes(mm(cells[...], spread_cells[...]), other, 5)
    for side in range(2):
        other[pl.ds(side * 5 + 4, KZT, stride=10), :] = jnp.zeros((KZT, 128), F32)


def middle_send_kernel(cells, wide_cells, sums, bias_sums, own, spread):
    fill_spread(wide_cells, OWN, spread)
    send_modes(mm(cells[...], spread[...]), own, 5)
    lane = lax.broadcasted_iota(jnp.int32, (C, ROWS), 1) >> 5
    picked = jnp.zeros((C, ROWS), F32)
    for k in range(8):
        picked = jnp.where(lane == k, sums[k * C : (k + 1) * C, :], picked)
    both = jnp.concatenate([picked, bias_sums[...], jnp.zeros((16, ROWS), F32)], axis=0)
    fold = ones_where((ROWS, 128), channel, lambda i: i, F32)
    folded = jnp.dot(both, fold, precision=HIGHEST, preferred_element_type=F32)
    for side in range(2):
        own[pl.ds(side * 5 + 4, KZT, stride=10), :] = folded


def last_own_kernel(
    own_in, modes, dmodes, wide_modes, depth_in,
    part, spread_other, depth, grad_out,
    spread, grad, sems,
):
    arriving = pltpu.make_async_copy(depth_in.at[pl.ds(0, 3 * KZT)], depth, sems.at[0])
    arriving.start()
    tiled = mm(wide_halves(by_mode(dmodes[...])), ones_where((2 * C, 128), channel, channel))
    expanded = mm(wide_halves(by_mode(modes[...])), ones_where((2 * C, C * C), channel, group))
    for j in range(8):
        grad[:, j * 128 : (j + 1) * 128] = expanded[:, j * 128 : (j + 1) * 128] * tiled
    leaving = pltpu.make_async_copy(grad, grad_out, sems.at[1])
    leaving.start()
    invert_own(own_in, 5, wide_modes, part, spread_other, spread)
    arriving.wait()
    leaving.wait()


def last_kernel(
    own_in, other_in, part, spread_other, dpre, depth, mixing,
    grad_out, grad_weight, grad_bias,
    grad, stack, sems,
):
    inverted = part[...] + mm(received_modes(other_in, 5).astype(BF16), spread_other[...])
    fill_stack(inverted, stack)
    total = own_in[pl.ds(4, KZT, stride=10), :] + other_in[pl.ds(4, KZT, stride=10), :]
    total = total * norm_scale
    grad_weight[...] = total[0:C, 0:C]
    grad_bias[...] = total[C : C + 1, 0:C]
    copies = [
        pltpu.make_async_copy(source, target, sems.at[i])
        for i, (source, target) in enumerate(block_pairs(grad, grad_out))
    ]
    for i in range(8):
        spectral = mm_tn(stack[i // 4, :, block_rows(i % 4)], depth[...])
        grad[block_rows(i), :] = (spectral + mm(mixing[...], dpre[block_rows(i), :])).astype(BF16)
        copies[i].start()
    for copy in copies:
        copy.wait()


HELD = pl.BlockSpec(memory_space=pltpu.VMEM)
FAR = pl.BlockSpec(memory_space=pltpu.HBM)
SMEM = pl.BlockSpec(memory_space=pltpu.SMEM)
PARAMS = pltpu.CompilerParams(vmem_limit_bytes=24 * 1024 * 1024)


SHORT = pl.CostEstimate(flops=2 * 10**9, bytes_accessed=4 * 10**6, transcendentals=0)
LONG = pl.CostEstimate(flops=10**10, bytes_accessed=2 * 10**7, transcendentals=0)


def like(*shape, dtype=F32):
    return jax.ShapeDtypeStruct(shape, dtype)


def call(kernel, name, ins, outs, out_shape, scratch=(), cost=None):
    return pl.pallas_call(
        kernel,
        name=name,
        in_specs=ins,
        out_specs=outs,
        out_shape=out_shape,
        scratch_shapes=list(scratch),
        compiler_params=PARAMS,
        cost_estimate=cost,
    )


def swap_cores(value):
    return lax.ppermute(value, "gy", [(i, i ^ 1) for i in range(GY)])


def exchange(messages, lines):
    groups = [[(g * 2 + side) * 2 + core for g in range(GX) for side in range(2)] for core in range(2)]
    shaped = messages.reshape(128, 1, lines * 128)
    moved = lax.all_to_all(
        shaped, ("gx", "gy"), split_axis=0, concat_axis=0, tiled=True, axis_index_groups=groups
    )
    return moved.reshape(128 * lines, 128)


def far(value):
    return pltpu.with_memory_space_constraint(value, pltpu.HBM)


def local(layer_input, cotangent, spectral_weight, bypass_weight, channel_bias, hash_key):
    table = {name: jnp.asarray(value) for name, value in tables().items()}
    gather, scatter = table["gather"], table["scatter"]
    depth, down_cells, down_modes = (far(table[name]) for name in ("depth", "down_cells", "down_modes"))
    weight = spectral_weight.reshape(ROWS, C * C)
    field = far(layer_input.reshape(-1, LZT))
    field_far = pltpu.HBM((2048, LZT), BF16)
    held = lambda *shape, dtype=BF16: pltpu.VMEM(shape, dtype)
    sems = lambda count: pltpu.SemaphoreType.DMA((count,))
    field_held = held(2048, LZT)
    flat = held(2, 4, KZT, ROWS, dtype=F32)
    down = held(GY, 32, 32)
    half_rows = held(512, 1024)
    half_columns = held(1024, 512)
    part_like = like(128, 1024)
    cells_like = like(128, 1024, dtype=BF16)
    spread_like = like(512, 1024, dtype=BF16)
    field_like = like(2048, LZT, dtype=BF16)

    other, cells, wide_cells = call(
        forward_kernel,
        "forward",
        [FAR] * 3,
        [HELD] * 3,
        [like(512, 128), cells_like, like(32, 1024)],
        [field_held, held(KZT, LZT), down, half_columns, flat, sems(10)],
    )(field, depth, down_cells)
    arriving = swap_cores(other)
    own = call(forward_own_kernel, "forward_own", [HELD] * 2, HELD, like(512, 128), [half_columns], cost=SHORT)(
        cells, wide_cells
    )
    messages = exchange(own + arriving, 4)

    mixing_like = like(ROWS, ROWS, dtype=BF16)
    prepared = call(
        prepare_kernel,
        "prepare",
        [SMEM, FAR, FAR, HELD, HELD],
        [HELD] * 5,
        [field_like, mixing_like, mixing_like, like(32, 1024), like(16, 1024, dtype=BF16)],
        [field_held, down, sems(8), sems(1)],
        LONG,
    )(hash_key, far(cotangent.reshape(-1, LZT)), down_modes, bypass_weight, channel_bias.reshape(1, C))
    messages, (kept, mixing, mixing_turned, wide_modes, wide_bias) = lax.optimization_barrier((messages, prepared))

    planes, modes = call(mix_kernel, "mix", [HELD] * 4, [HELD] * 2, [like(512, 128), like(KX, ROWS)])(
        messages, weight, gather, scatter
    )
    own_cells = exchange(planes, 4)
    other_cells = swap_cores(own_cells)
    part, spread_other, spread_cells, field_near, depth_near = call(
        middle_own_kernel,
        "middle_own",
        [HELD] * 3 + [FAR] * 2,
        [HELD] * 5,
        [
            part_like, spread_like, like(1024, 512, dtype=BF16), like(8, KZT + ROWS + 16, LZT, dtype=BF16),
            like(3 * KZT + 16, LZT, dtype=BF16),
        ],
        [half_rows, sems(9)],
        SHORT,
    )(own_cells, wide_modes, wide_cells, field, depth)

    preact = held(ROWS, LZT, dtype=F32)
    other, cells, sums, bias_sums, dpre = call(
        middle_kernel,
        "middle",
        [HELD] * 9,
        [HELD] * 5,
        [like(640, 128), cells_like, like(ROWS, ROWS), like(16, ROWS), field_like],
        [held(2, 3 * KZT + 16, 1024), preact, preact, flat],
    )(
        other_cells, part, spread_other, spread_cells, field_near, kept, depth_near,
        wide_bias, mixing_turned,
    )
    arriving = swap_cores(other)
    own = call(middle_send_kernel, "middle_send", [HELD] * 4, HELD, like(640, 128), [half_columns], SHORT)(
        cells, wide_cells, sums, bias_sums
    )
    messages = exchange(own + arriving, 5)

    planes, dmodes = call(back_kernel, "back", [HELD] * 4, [HELD] * 2, [like(640, 128), like(KX, ROWS)])(
        messages, weight, gather, scatter
    )
    own_cells = exchange(planes, 5)
    other_cells = swap_cores(own_cells)
    part, spread_other, depth_near, grad_spectral = call(
        last_own_kernel,
        "last_own",
        [HELD] * 4 + [FAR],
        [HELD] * 3 + [FAR],
        [part_like, spread_like, like(3 * KZT, LZT, dtype=BF16), pltpu.HBM((ROWS, 1024), F32)],
        [half_rows, held(ROWS, 1024, dtype=F32), sems(2)],
        SHORT,
    )(own_cells, modes, dmodes, wide_modes, depth)

    grad_input, grad_weight, grad_bias = call(
        last_kernel,
        "last",
        [HELD] * 7,
        [FAR, HELD, HELD],
        [field_far, like(C, C), like(1, C)],
        [field_held, held(2, 3 * KZT, 1024), sems(8)],
    )(own_cells, other_cells, part, spread_other, dpre, depth_near, mixing)
    return (
        grad_input.reshape(layer_input.shape),
        grad_spectral.reshape(spectral_weight.shape),
        grad_weight,
        grad_bias.reshape(C),
    )


def solution(mesh):
    return jax.shard_map(
        local,
        mesh=mesh,
        in_specs=(
            P("gx", "gy", None, None),
            P("gx", "gy", None, None),
            P("gy", "gx", None, None),
            P(),
            P(),
            P(),
        ),
        out_specs=(P("gx", "gy", None, None), P("gy", "gx", None, None), P(), P()),
        check_vma=False,
    )
```
